32 devices in a mesh: dp: 2 (over core), vocab: 16 (over z, y, x).
Axes of the slice: x: 2, y: 2, z: 4, core: 2. Of those that a mesh axis runs over, the one named last changes fastest.
Arguments:
- mentor_score_matrix: bfloat16 [512, 30720], P('dp', 'vocab'), may hold values from -12 to 512
- learner_score_matrix: bfloat16 [512, 65536], P('dp', 'vocab'), may hold values from -12 to 512
- align_dev: int32 [480, 2], P('vocab'), may hold values from 0 to 15, all different within a row; in each aligned block of 30 rows (0 to 29, 30 to 59, ...) at most 5 rows name the same one
- align_slot: int32 [480, 2], P('vocab'), may hold values from 0 to 63
- align_weight: bfloat16 [480, 2, 4096], P('vocab'), may hold values from 0.00077819824 to 0.015625
Outputs:
- scaled_grad: bfloat16 [512, 65536], P('dp', 'vocab')
- divergence_penalty_result: float32 [], replicated
The draws below stay inside these ranges and needn't reach their ends.
Inputs may be any that keep to these rules, and one draw needn't show every extreme that they name: `align_dev`: the 30 teacher blocks of one vocab shard name each owner at most 5 times in all, and in every draw some shard names some owner exactly 5 times; the 2 owners of one teacher block differ.
All inputs are finite; a program needn't handle non-finite values.
Results may differ from the reference program's by a relative error of at most 0.0039.
Values may be sent and summed in bfloat16 or wider, within the bound.
A program may use at most 64 MiB of HBM per device.

```python
import math
import jax
import jax.numpy as jnp
import numpy as np
from jax import lax

BLK = 64
TB_DEV = 30
SB_DEV = 64
TOPK = 2
SMOOTHING_HEAT = 2
TB = 480
SB = 1024
VT = 30720
VS = 65536
SYMBOL_NUMBER = 512
MOST = 5
N_VOCAB = 16


def logit_field(key, row_count, col_count, ramp_low):
    noise_draw = jnp.clip(jax.random.normal(jax.random.fold_in(key, 11), (row_count, col_count), jnp.float32), -4.0, 4.0)
    column_place = jnp.arange(col_count, dtype=jnp.float32)[None, :] / float(col_count)
    return 3.0 * noise_draw + ramp_low * column_place


def draw_mentor_score_matrix(key, part):
    return logit_field(jax.random.fold_in(key, 21), SYMBOL_NUMBER, VT, 3.6).astype(jnp.bfloat16)


def draw_learner_score_matrix(key, part):
    return logit_field(jax.random.fold_in(key, 22), SYMBOL_NUMBER, VS, 0.0).astype(jnp.bfloat16)


def place_ends(entries, own_key, smallest, largest):
    longest = entries.shape.index(max(entries.shape))
    spots = []
    for shift in (0, 1):
        where = [jax.random.randint(jax.random.fold_in(own_key, axis), (), 0, length) for axis, length in enumerate(entries.shape)]
        where[longest] = (where[longest] + shift) % entries.shape[longest]
        spots.append(tuple(where))
    return entries.at[spots[0]].set(smallest).at[spots[1]].set(largest)


def block_scale(stream_key, shape, shards, least, largest):
    factor_of = 1.0
    for axis_at, blocks in shards:
        steps = jax.random.uniform(jax.random.fold_in(jax.random.fold_in(stream_key, 6), axis_at), (blocks,), jnp.float32, least / len(shards), largest / len(shards))
        factor_of = factor_of * jnp.repeat(jnp.exp(steps), shape[axis_at] // blocks).reshape((-1,) + (1,) * (len(shape) - 1 - axis_at))
    return factor_of


def routed_block(rng, own, number, rows, number_of, top, most, skew):
    sequence = jax.random.permutation(rng, number_of)
    crowded, ordinary = shares(number_of, rows * top, most, skew, True), shares(number_of, rows * top, most, skew, False)
    places = jnp.arange(number_of)

    def named(tallies, rotation):
        used = int((tallies > 0).sum())
        fixed = max(1, used // 4)
        moved = fixed + (places - fixed + rotation * (used - fixed)) % max(1, number_of - fixed)
        return jnp.zeros((number_of,), jnp.int32).at[sequence[jnp.where(places < fixed, places, moved)]].set(jnp.asarray(tallies, jnp.int32))

    tallies = jnp.where(number % 4 == 0, named(crowded, number // 4), named(ordinary, number - number // 4 - 1))
    mixed = jax.random.permutation(jax.random.fold_in(own, 3), number_of)
    giver, sink = mixed[0:number_of // 2 * 2:2], mixed[1:number_of // 2 * 2:2]
    slack = jnp.minimum(tallies[giver] - 1, most - tallies[sink]) // 2
    slack = jnp.where((giver == sequence[0]) | (sink == sequence[0]) | (tallies[sink] == 0), 0, jnp.maximum(slack, 0))
    moved = jax.random.randint(jax.random.fold_in(own, 4), (number_of // 2,), 0, 1 << 20) % (slack + 1)
    tallies = tallies.at[giver].add(-moved).at[sink].add(moved)
    items = jnp.searchsorted(jnp.cumsum(tallies), jnp.arange(rows * top), side="right").astype(jnp.int32)
    table = items.reshape(top, rows).T
    table = table[jax.random.permutation(jax.random.fold_in(own, 1), rows)]
    rotation = jax.random.randint(jax.random.fold_in(own, 2), (rows, 1), 0, top)
    return jnp.take_along_axis(table, (jnp.arange(top)[None, :] + rotation) % top, axis=1)


def shares(amount, total, reach, lean, full):
    loads = [(1 << 20) // math.isqrt(grade ** lean) + 1 for grade in range(1, amount + 1)]
    largest = reach if full else min(reach, max(-(-total // amount), total * loads[0] // sum(loads)))
    least = 1 if total - largest >= amount - 1 else 0
    given, surplus = [largest] + [least] * (amount - 1), total - largest - least * (amount - 1)
    while surplus > 0:
        movable = [i for i in range(1, amount) if given[i] < largest] or [i for i in range(1, amount) if given[i] < reach]
        whole, remaining = sum([loads[i] for i in movable]), surplus
        for i in movable:
            extra = min(reach - given[i], max(1, remaining * loads[i] // whole), surplus)
            given[i] = given[i] + extra
            surplus = surplus - extra
    return np.array(given)


def setup_inputs(seed: int = 0) -> dict:
    seeds = jax.random.split(jax.random.key(seed), 6)
    mentor_score_matrix = draw_mentor_score_matrix(jax.random.fold_in(seeds[5], 71), 0)
    learner_score_matrix = draw_learner_score_matrix(jax.random.fold_in(seeds[5], 71), 0)
    align_dev_keys = jax.random.split(jax.random.fold_in(seeds[2], 1), TB // TB_DEV)
    align_dev_turns = jax.random.permutation(jax.random.fold_in(seeds[2], 3), TB // TB_DEV)
    align_dev = jax.vmap(lambda own, number: routed_block(jax.random.fold_in(seeds[2], 2), own, number, TB_DEV, N_VOCAB, TOPK, MOST, 2))(align_dev_keys, align_dev_turns).reshape((TB, TOPK))
    align_slot = place_ends(jax.random.randint(seeds[3], (TB, TOPK), 0, SB_DEV), jax.random.fold_in(seeds[3], 1), 0, SB_DEV - 1).astype(jnp.int32)
    align_weight = jnp.clip(jnp.exp(math.log(0.015625) - 2.9996462 * jax.random.uniform(seeds[4], (TB, TOPK, BLK * BLK), jnp.float32) ** block_scale(seeds[4], (TB, TOPK, BLK * BLK), ((0, 16),), -0.2, 0.2)), 0.00077819824, 0.015625).astype(jnp.bfloat16)
    return {"mentor_score_matrix": mentor_score_matrix, "learner_score_matrix": learner_score_matrix, "align_dev": align_dev, "align_slot": align_slot, "align_weight": align_weight}


def reference(mentor_score_matrix, learner_score_matrix, align_dev, align_slot, align_weight):
    smoothing_heat_value = float(SMOOTHING_HEAT)
    mentor_smoothed_scores = mentor_score_matrix.astype(jnp.float32) / smoothing_heat_value
    teacher_high = jnp.max(mentor_smoothed_scores, axis=1, keepdims=True)
    teacher_lse = teacher_high + jnp.log(jnp.sum(jnp.exp(mentor_smoothed_scores - teacher_high), axis=1, keepdims=True))
    teacher_probs = jnp.exp(mentor_smoothed_scores - teacher_lse).astype(jnp.bfloat16)
    row_count = teacher_probs.shape[0]
    prob_blocks = teacher_probs.astype(jnp.float32).reshape(row_count, TB, BLK)
    weight_blocks = align_weight.astype(jnp.float32).reshape(TB, TOPK, BLK, BLK)
    target_block = (align_dev * SB_DEV + align_slot).astype(jnp.int32)
    target_mass = jnp.zeros((row_count, SB, BLK), jnp.float32)
    for pick_index in range(TOPK):
        contrib = jnp.einsum("rbc,bcd->rbd", prob_blocks, weight_blocks[:, pick_index], precision=lax.Precision.HIGHEST)
        rounded = lax.optimization_barrier(contrib.astype(jnp.bfloat16))
        target_mass = target_mass.at[:, target_block[:, pick_index]].add(rounded.astype(jnp.float32))
    target = target_mass.reshape(row_count, VS)
    target_total = jnp.sum(target, axis=1, keepdims=True)
    learner_smoothed_scores = learner_score_matrix.astype(jnp.float32) / smoothing_heat_value
    student_high = jnp.max(learner_smoothed_scores, axis=1, keepdims=True)
    student_lse = student_high + jnp.log(jnp.sum(jnp.exp(learner_smoothed_scores - student_high), axis=1, keepdims=True))
    student_logprob = learner_smoothed_scores - student_lse
    scaled_grad = (float(VS) * (target_total * jnp.exp(student_logprob) - target)).astype(jnp.bfloat16)
    symbolwise_penalty = jax.scipy.special.xlogy(target, target) - target * student_logprob
    divergence_penalty_result = smoothing_heat_value * smoothing_heat_value * jnp.sum(symbolwise_penalty) / float(SYMBOL_NUMBER)
    return scaled_grad, divergence_penalty_result
```

```python
import functools

import jax
import jax.numpy as jnp
from jax import lax
from jax.experimental import pallas as pl
from jax.experimental.pallas import tpu as pltpu
from jax.sharding import PartitionSpec as P

BLK = 64
SMOOTHING_HEAT = 2
LANES = 128
STATS = 8
CODE_ROW = 5
VMEM_BYTES = 48 * 1024 * 1024
MESH = pl.DeviceIdType.MESH


def low_lanes(shape):
    return lax.broadcasted_iota(jnp.int32, shape, len(shape) - 1) < BLK


def columns_to_rows(columns, first, count):
    rows = columns[0].shape[0]
    lane = lax.broadcasted_iota(jnp.int32, (rows, LANES), 1)
    table = jnp.zeros((rows, LANES), jnp.float32)
    for at, column in enumerate(columns):
        table = jnp.where(lane == first + at, column, table)
    return jnp.transpose(table)[:count]


def teacher_kernel(owners, most, dev_ref, slot_ref, mentor_ref, weight_ref, out_ref, stats_ref, count_ref, place_ref):
    row_count, width = mentor_ref.shape
    half = row_count // 2
    topk = dev_ref.shape[1]
    tb_local = dev_ref.shape[0]

    for owner in range(owners):
        count_ref[owner] = 0
    code_lane = lax.broadcasted_iota(jnp.int32, (1, row_count), 1)

    def place(b, codes):
        for k in range(topk):
            owner = dev_ref[b, k]
            earlier = count_ref[owner]
            count_ref[owner] = earlier + 1
            position = owner * most + earlier
            place_ref[b * topk + k] = position
            codes = jnp.where(code_lane == position, slot_ref[b, k].astype(jnp.float32), codes)
        return codes

    codes = lax.fori_loop(0, tb_local, place, jnp.full((1, row_count), -1.0, jnp.float32))

    tiles = width // LANES
    high = mentor_ref[:, :LANES]
    for tile in range(1, tiles):
        high = jnp.maximum(high, mentor_ref[:, tile * LANES:(tile + 1) * LANES])
    high = jnp.max(high.astype(jnp.float32), axis=1, keepdims=True) / float(SMOOTHING_HEAT)

    low = low_lanes((BLK, LANES))
    none = jnp.zeros((BLK, LANES), jnp.bfloat16)

    def pair(j, carry):
        total, mass = carry
        x = mentor_ref[:, pl.ds(pl.multiple_of(j * LANES, LANES), LANES)].astype(jnp.float32)
        e = jnp.exp(x / float(SMOOTHING_HEAT) - high)
        total = total + e
        e = e.astype(jnp.bfloat16)
        lhs = jnp.concatenate([e[:half], e[half:]], axis=1)
        lefts, rights = [], []
        for b in range(2):
            blocks = [weight_ref[(2 * j + b) * topk + k] for k in range(topk)]
            pad_before, pad_after = [none] * (topk * b), [none] * (topk * (1 - b))
            lefts.append(jnp.concatenate(pad_before + [jnp.where(low, w, none) for w in blocks] + pad_after, axis=1))
            rights.append(jnp.concatenate(pad_before + [jnp.where(low, none, w) for w in blocks] + pad_after, axis=1))
        rhs = jnp.concatenate(lefts + rights, axis=0)
        terms = jnp.dot(lhs, rhs, preferred_element_type=jnp.float32).astype(jnp.bfloat16)
        for at in range(2 * topk):
            term = terms[:, at * LANES:(at + 1) * LANES]
            out_ref[place_ref[2 * topk * j + at]] = term
            mass = mass + term.astype(jnp.float32)
        return total, mass

    total, mass = lax.fori_loop(
        0, tiles, pair,
        (jnp.zeros((row_count, LANES), jnp.float32), jnp.zeros((half, LANES), jnp.float32)),
    )
    low = low_lanes((half, LANES))
    mass = jnp.concatenate([
        jnp.sum(jnp.where(low, mass, 0.0), axis=1, keepdims=True),
        jnp.sum(jnp.where(low, 0.0, mass), axis=1, keepdims=True),
    ], axis=0)
    total = jnp.sum(total, axis=1, keepdims=True)
    rows = columns_to_rows([high, total, mass], 0, STATS)
    row = lax.broadcasted_iota(jnp.int32, (STATS, row_count), 0)
    stats_ref[...] = jnp.where(row == CODE_ROW, codes, rows)


def exchange_kernel(owners, out_ref, stats_ref, learner_ref, recv_ref, cols_ref, codes_ref,
                    learner, message, table, send, recv, small_send, small_recv, local):
    dp, me = lax.axis_index("dp"), lax.axis_index("vocab")
    row_count = learner.shape[0]
    load = pltpu.make_async_copy(learner_ref, learner, local.at[0])
    load.start()
    own = pltpu.make_async_copy(out_ref.at[me], recv_ref.at[me], local.at[1])
    own.start()

    barrier = pltpu.get_barrier_semaphore()

    def greet(k, carry):
        pl.semaphore_signal(barrier, inc=1, device_id=(dp, lax.rem(me + k, owners)), device_id_type=MESH)
        return carry

    lax.fori_loop(1, owners, greet, 0)
    pl.semaphore_wait(barrier, owners - 1)

    def block_copy(k):
        peer = lax.rem(me + k, owners)
        return pltpu.make_async_remote_copy(
            src_ref=out_ref.at[peer], dst_ref=recv_ref.at[me], send_sem=send.at[k], recv_sem=recv.at[k],
            device_id=(dp, peer), device_id_type=MESH)

    def small_copy(k):
        peer = lax.rem(me + k, owners)
        return pltpu.make_async_remote_copy(
            src_ref=message, dst_ref=table.at[me], send_sem=small_send.at[k], recv_sem=small_recv.at[k],
            device_id=(dp, peer), device_id_type=MESH)

    def start_block(k, carry):
        block_copy(k).start()
        return carry

    lax.fori_loop(1, owners, start_block, 0)

    load.wait()
    tiles = learner.shape[1] // LANES

    def tile_of(j):
        return learner[:, pl.ds(pl.multiple_of(j * LANES, LANES), LANES)]

    high = lax.fori_loop(1, tiles, lambda j, h: jnp.maximum(h, tile_of(j)), learner[:, :LANES])
    high = jnp.max(high.astype(jnp.float32), axis=1, keepdims=True) / float(SMOOTHING_HEAT)

    def add_exp(j, total):
        return total + jnp.exp(tile_of(j).astype(jnp.float32) / float(SMOOTHING_HEAT) - high)

    total = lax.fori_loop(0, tiles, add_exp, jnp.zeros((row_count, LANES), jnp.float32))
    total = jnp.sum(total, axis=1, keepdims=True)
    message[...] = stats_ref[...] + columns_to_rows([high, total], 3, STATS)
    table[me] = message[...]

    def start_small(k, carry):
        small_copy(k).start()
        return carry

    def wait_small(k, carry):
        small_copy(k).wait()
        return carry

    lax.fori_loop(1, owners, start_small, 0)
    lax.fori_loop(1, owners, wait_small, 0)

    teacher_high = table[:, 0, :]
    teacher_scale = jnp.exp(teacher_high - jnp.max(teacher_high, axis=0, keepdims=True))
    weight = teacher_scale / jnp.sum(table[:, 1, :] * teacher_scale, axis=0, keepdims=True)
    target_total = jnp.sum(table[:, 2, :] * weight, axis=0, keepdims=True)
    student_high = table[:, 3, :]
    top = jnp.max(student_high, axis=0, keepdims=True)
    student_lse = top + jnp.log(jnp.sum(table[:, 4, :] * jnp.exp(student_high - top), axis=0, keepdims=True))
    fill = jnp.zeros((LANES - owners - STATS, row_count), jnp.float32)
    row = lax.broadcasted_iota(jnp.int32, (STATS, row_count), 0)
    tail = jnp.where(row == 0, target_total, jnp.where(row == 1, student_lse, 0.0))
    cols_ref[...] = jnp.transpose(jnp.concatenate([weight, tail, fill], axis=0))
    codes_ref[...] = table[:, CODE_ROW, :]

    def wait_block(k, carry):
        block_copy(k).wait()
        return carry

    lax.fori_loop(1, owners, wait_block, 0)
    own.wait()


def student_kernel(owners, most, codes_ref, recv_ref, cols_ref, learner_ref, grad_ref, loss_ref, target_ref):
    me = lax.axis_index("vocab")
    row_count, width = learner_ref.shape
    half = row_count // 2
    sb_local = width // BLK
    vocab_width = float(width * owners)

    def clear(c, carry):
        target_ref[c] = jnp.zeros((half, LANES), jnp.float32)
        return carry

    lax.fori_loop(0, sb_local, clear, 0)
    low = low_lanes((half, LANES))
    for source in range(owners):
        column = cols_ref[:, source:source + 1]
        scale = jnp.where(low, column[:half], column[half:])
        for at in range(most):
            code = codes_ref[source, me * most + at].astype(jnp.int32)
            block = jnp.where(code < 0, sb_local, code)
            target_ref[block] = target_ref[block] + recv_ref[source, at].astype(jnp.float32) * scale

    target_total = cols_ref[:, owners:owners + 1] * vocab_width
    lse = cols_ref[:, owners + 1:owners + 2]

    def pair(j, loss):
        first, second = target_ref[2 * j], target_ref[2 * j + 1]
        target = jnp.concatenate([
            jnp.where(low, first, pltpu.roll(second, BLK, 1)),
            jnp.where(low, pltpu.roll(first, BLK, 1), second),
        ], axis=0)
        at = pl.ds(pl.multiple_of(j * LANES, LANES), LANES)
        logprob = learner_ref[:, at].astype(jnp.float32) / float(SMOOTHING_HEAT) - lse
        grad_ref[:, at] = (target_total * jnp.exp(logprob) - vocab_width * target).astype(jnp.bfloat16)
        fed = target > 0.0
        return loss + jnp.where(fed, target * (jnp.log(jnp.where(fed, target, 1.0)) - logprob), 0.0)

    loss = lax.fori_loop(0, sb_local // 2, pair, jnp.zeros((row_count, LANES), jnp.float32))
    loss_ref[...] = jnp.sum(loss.reshape(row_count // 8, 8, LANES), axis=0)


def loss_kernel(parts, owners, scale, loss_ref, result_ref, table, send, recv):
    me = lax.axis_index("dp") * owners + lax.axis_index("vocab")
    everyone = parts * owners

    def device(k):
        peer = lax.rem(me + k, everyone)
        return (peer // owners, lax.rem(peer, owners))

    barrier = pltpu.get_barrier_semaphore()

    def greet(k, carry):
        pl.semaphore_signal(barrier, inc=1, device_id=device(k), device_id_type=MESH)
        return carry

    lax.fori_loop(1, everyone, greet, 0)
    table[me] = loss_ref[...]
    pl.semaphore_wait(barrier, everyone - 1)

    def copy(k):
        return pltpu.make_async_remote_copy(
            src_ref=loss_ref, dst_ref=table.at[me], send_sem=send.at[k], recv_sem=recv.at[k],
            device_id=device(k), device_id_type=MESH)

    def start(k, carry):
        copy(k).start()
        return carry

    def wait(k, carry):
        copy(k).wait()
        return carry

    lax.fori_loop(1, everyone, start, 0)
    lax.fori_loop(1, everyone, wait, 0)
    total = jnp.sum(table[...], axis=0)
    total = jnp.sum(jnp.sum(total, axis=0, keepdims=True), axis=1, keepdims=True)
    result_ref[...] = total * scale


def per_device(mentor_score_matrix, learner_score_matrix, align_dev, align_slot, align_weight):
    parts, owners = lax.axis_size("dp"), lax.axis_size("vocab")
    row_count, _ = mentor_score_matrix.shape
    half = row_count // 2
    tb_local, topk = align_dev.shape
    most = max(2, 3 * tb_local * topk // (2 * owners))
    width = learner_score_matrix.shape[1]
    sb_local = width // BLK
    vmem = pl.BlockSpec(memory_space=pltpu.VMEM)
    smem = pl.BlockSpec(memory_space=pltpu.SMEM)
    anywhere = pl.BlockSpec(memory_space=pl.ANY)

    weight = align_weight.reshape(tb_local * topk, BLK, BLK)
    weight = jnp.concatenate([weight, weight], axis=2)

    outgoing, stats = pl.pallas_call(
        functools.partial(teacher_kernel, owners, most),
        out_shape=(
            jax.ShapeDtypeStruct((owners * most, half, LANES), jnp.bfloat16),
            jax.ShapeDtypeStruct((STATS, row_count), jnp.float32),
        ),
        in_specs=[smem, smem, vmem, vmem],
        out_specs=(vmem, vmem),
        scratch_shapes=[pltpu.SMEM((owners,), jnp.int32), pltpu.SMEM((tb_local * topk,), jnp.int32)],
        compiler_params=pltpu.CompilerParams(vmem_limit_bytes=VMEM_BYTES),
        name="teacher_terms",
    )(align_dev, align_slot, mentor_score_matrix, weight)

    arrived, columns, codes = pl.pallas_call(
        functools.partial(exchange_kernel, owners),
        out_shape=(
            jax.ShapeDtypeStruct((owners, most, half, LANES), jnp.bfloat16),
            jax.ShapeDtypeStruct((row_count, LANES), jnp.float32),
            jax.ShapeDtypeStruct((owners, row_count), jnp.float32),
        ),
        in_specs=[anywhere, vmem, anywhere],
        out_specs=(anywhere, vmem, vmem),
        scratch_shapes=[
            pltpu.VMEM((row_count, width), jnp.bfloat16),
            pltpu.VMEM((STATS, row_count), jnp.float32),
            pltpu.VMEM((owners, STATS, row_count), jnp.float32),
            pltpu.SemaphoreType.DMA((owners,)),
            pltpu.SemaphoreType.DMA((owners,)),
            pltpu.SemaphoreType.DMA((owners,)),
            pltpu.SemaphoreType.DMA((owners,)),
            pltpu.SemaphoreType.DMA((2,)),
        ],
        compiler_params=pltpu.CompilerParams(
            collective_id=0, has_side_effects=True, vmem_limit_bytes=VMEM_BYTES),
        name="exchange",
    )(outgoing.reshape(owners, most, half, LANES), stats, learner_score_matrix)

    scaled_grad, loss = pl.pallas_call(
        functools.partial(student_kernel, owners, most),
        out_shape=(
            jax.ShapeDtypeStruct((row_count, width), jnp.bfloat16),
            jax.ShapeDtypeStruct((8, LANES), jnp.float32),
        ),
        in_specs=[smem, vmem, vmem, vmem],
        out_specs=(vmem, vmem),
        scratch_shapes=[pltpu.VMEM((sb_local + 1, half, LANES), jnp.float32)],
        compiler_params=pltpu.CompilerParams(vmem_limit_bytes=VMEM_BYTES),
        name="student_gradient",
    )(codes, arrived, columns, learner_score_matrix)

    scale = float(SMOOTHING_HEAT) * float(SMOOTHING_HEAT) / float(row_count * parts)
    total = pl.pallas_call(
        functools.partial(loss_kernel, parts, owners, scale),
        out_shape=jax.ShapeDtypeStruct((1, 1), jnp.float32),
        in_specs=[vmem],
        out_specs=vmem,
        scratch_shapes=[
            pltpu.VMEM((parts * owners, 8, LANES), jnp.float32),
            pltpu.SemaphoreType.DMA((parts * owners,)),
            pltpu.SemaphoreType.DMA((parts * owners,)),
        ],
        compiler_params=pltpu.CompilerParams(collective_id=1, has_side_effects=True),
        name="loss_sum",
    )(loss)
    return scaled_grad, total[0, 0]


def solution(mesh):
    in_specs = (
        P("dp", "vocab"),
        P("dp", "vocab"),
        P("vocab", None),
        P("vocab", None),
        P("vocab", None, None),
    )
    out_specs = (P("dp", "vocab"), P())
    return jax.shard_map(
        per_device, mesh=mesh, in_specs=in_specs, out_specs=out_specs, check_vma=False
    )
```

```python
import functools

import jax
import jax.numpy as jnp
from jax import lax
from jax.experimental import pallas as pl
from jax.experimental.pallas import tpu as pltpu
from jax.sharding import PartitionSpec as P

BLK = 64
SMOOTHING_HEAT = 2
LANES = 128
STATS = 8
CODE_ROW = 5
OUTER = 4
VMEM_BYTES = 24 * 1024 * 1024
MESH = pl.DeviceIdType.MESH


def low_lanes(shape):
    return lax.broadcasted_iota(jnp.int32, shape, len(shape) - 1) < BLK


def columns_to_rows(columns, first, count):
    rows = columns[0].shape[0]
    lane = lax.broadcasted_iota(jnp.int32, (rows, LANES), 1)
    table = jnp.zeros((rows, LANES), jnp.float32)
    for at, column in enumerate(columns):
        table = jnp.where(lane == first + at, column, table)
    return jnp.transpose(table)[:count]


def teacher_kernel(owners, most, dev_ref, slot_ref, mentor_ref, weight_ref, out_ref, stats_ref, count_ref, place_ref):
    row_count, width = mentor_ref.shape
    half = row_count // 2
    topk = dev_ref.shape[0]
    tb_local = dev_ref.shape[1]

    for owner in range(owners):
        count_ref[owner] = 0
    code_lane = lax.broadcasted_iota(jnp.int32, (1, row_count), 1)

    def place(b, codes):
        for k in range(topk):
            owner = dev_ref[k, b]
            earlier = count_ref[owner]
            count_ref[owner] = earlier + 1
            position = owner * most + earlier
            place_ref[b * topk + k] = position
            codes = jnp.where(code_lane == position, slot_ref[k, b].astype(jnp.float32), codes)
        return codes

    codes = lax.fori_loop(0, tb_local, place, jnp.full((1, row_count), -1.0, jnp.float32))

    tiles = width // LANES
    high = mentor_ref[:, :LANES]
    for tile in range(1, tiles):
        high = jnp.maximum(high, mentor_ref[:, tile * LANES:(tile + 1) * LANES])
    high = jnp.max(high.astype(jnp.float32), axis=1, keepdims=True) / float(SMOOTHING_HEAT)

    low = low_lanes((BLK, LANES))
    none = jnp.zeros((BLK, LANES), jnp.bfloat16)

    def pair(j, carry):
        total, mass = carry
        x = mentor_ref[:, pl.ds(pl.multiple_of(j * LANES, LANES), LANES)].astype(jnp.float32)
        e = jnp.exp(x / float(SMOOTHING_HEAT) - high)
        total = total + e
        e = e.astype(jnp.bfloat16)
        lhs = jnp.concatenate([e[:half], e[half:]], axis=1)
        lefts, rights = [], []
        for b in range(2):
            blocks = [weight_ref[(2 * j + b) * topk + k] for k in range(topk)]
            pad_before, pad_after = [none] * (topk * b), [none] * (topk * (1 - b))
            lefts.append(jnp.concatenate(pad_before + [jnp.where(low, w, none) for w in blocks] + pad_after, axis=1))
            rights.append(jnp.concatenate(pad_before + [jnp.where(low, none, w) for w in blocks] + pad_after, axis=1))
        rhs = jnp.concatenate(lefts + rights, axis=0)
        terms = jnp.dot(lhs, rhs, preferred_element_type=jnp.float32).astype(jnp.bfloat16)
        for at in range(2 * topk):
            term = terms[:, at * LANES:(at + 1) * LANES]
            out_ref[place_ref[2 * topk * j + at]] = term
            mass = mass + term.astype(jnp.float32)
        return total, mass

    total, mass = lax.fori_loop(
        0, tiles, pair,
        (jnp.zeros((row_count, LANES), jnp.float32), jnp.zeros((half, LANES), jnp.float32)),
    )
    low = low_lanes((half, LANES))
    mass = jnp.concatenate([
        jnp.sum(jnp.where(low, mass, 0.0), axis=1, keepdims=True),
        jnp.sum(jnp.where(low, 0.0, mass), axis=1, keepdims=True),
    ], axis=0)
    total = jnp.sum(total, axis=1, keepdims=True)
    rows = columns_to_rows([high, total, mass], 0, STATS)
    row = lax.broadcasted_iota(jnp.int32, (STATS, row_count), 0)
    stats_ref[...] = jnp.where(row == CODE_ROW, codes, rows)


def outer_partner(outer, far):
    return (outer, outer + 1 - 2 * lax.rem(outer, 2), lax.rem(outer + 2, OUTER), OUTER - 1 - outer)[far]


def partner_copy(owners, dp, me, out_ref, recv_ref, send, recv, far, near):
    inner = owners // OUTER
    peer = outer_partner(me // inner, far) * inner + lax.rem(lax.rem(me, inner) + near, inner)
    slot = far * inner + near
    return pltpu.make_async_remote_copy(
        src_ref=out_ref.at[peer], dst_ref=recv_ref.at[me], send_sem=send.at[slot], recv_sem=recv.at[slot],
        device_id=(dp, peer), device_id_type=MESH)


def exchange_kernel(owners, out_ref, stats_ref, learner_ref, recv_ref, cols_ref, codes_ref,
                    learner, message, table, send, recv, small_send, small_recv, local):
    dp, me = lax.axis_index("dp"), lax.axis_index("vocab")
    row_count = learner.shape[0]
    load = pltpu.make_async_copy(learner_ref, learner, local.at[0])
    load.start()
    own = pltpu.make_async_copy(out_ref.at[me], recv_ref.at[me], local.at[1])
    own.start()

    barrier = pltpu.get_barrier_semaphore()

    def greet(k, carry):
        pl.semaphore_signal(barrier, inc=1, device_id=(dp, lax.rem(me + k, owners)), device_id_type=MESH)
        return carry

    lax.fori_loop(1, owners, greet, 0)
    pl.semaphore_wait(barrier, owners - 1)

    block_copy = functools.partial(partner_copy, owners, dp, me, out_ref, recv_ref, send, recv)

    def small_copy(k):
        peer = lax.rem(me + k, owners)
        return pltpu.make_async_remote_copy(
            src_ref=message, dst_ref=table.at[me], send_sem=small_send.at[k], recv_sem=small_recv.at[k],
            device_id=(dp, peer), device_id_type=MESH)

    def start_blocks(near, carry):
        block_copy(2, near).start()
        block_copy(1, near).start()
        block_copy(3, near).start()
        block_copy(0, near).start()
        return carry

    for far in (2, 1, 3):
        block_copy(far, 0).start()
    lax.fori_loop(1, owners // OUTER, start_blocks, 0)

    load.wait()
    tiles = learner.shape[1] // LANES

    def tile_of(j):
        return learner[:, pl.ds(pl.multiple_of(j * LANES, LANES), LANES)]

    high = lax.fori_loop(1, tiles, lambda j, h: jnp.maximum(h, tile_of(j)), learner[:, :LANES])
    high = jnp.max(high.astype(jnp.float32), axis=1, keepdims=True) / float(SMOOTHING_HEAT)

    def add_exp(j, total):
        return total + jnp.exp(tile_of(j).astype(jnp.float32) / float(SMOOTHING_HEAT) - high)

    total = lax.fori_loop(0, tiles, add_exp, jnp.zeros((row_count, LANES), jnp.float32))
    total = jnp.sum(total, axis=1, keepdims=True)
    message[...] = stats_ref[...] + columns_to_rows([high, total], 3, STATS)
    table[me] = message[...]

    def start_small(k, carry):
        small_copy(k).start()
        return carry

    def wait_small(k, carry):
        small_copy(k).wait()
        return carry

    lax.fori_loop(1, owners, start_small, 0)
    lax.fori_loop(1, owners, wait_small, 0)

    teacher_high = table[:, 0, :]
    teacher_scale = jnp.exp(teacher_high - jnp.max(teacher_high, axis=0, keepdims=True))
    weight = teacher_scale / jnp.sum(table[:, 1, :] * teacher_scale, axis=0, keepdims=True)
    target_total = jnp.sum(table[:, 2, :] * weight, axis=0, keepdims=True)
    student_high = table[:, 3, :]
    top = jnp.max(student_high, axis=0, keepdims=True)
    student_lse = top + jnp.log(jnp.sum(table[:, 4, :] * jnp.exp(student_high - top), axis=0, keepdims=True))
    fill = jnp.zeros((LANES - owners - STATS, row_count), jnp.float32)
    row = lax.broadcasted_iota(jnp.int32, (STATS, row_count), 0)
    tail = jnp.where(row == 0, target_total, jnp.where(row == 1, student_lse, 0.0))
    cols_ref[...] = jnp.transpose(jnp.concatenate([weight, tail, fill], axis=0))
    codes_ref[...] = table[:, CODE_ROW, :]

    def wait_blocks(near, carry):
        for far in range(OUTER):
            block_copy(far, near).wait()
        return carry

    for far in (2, 1, 3):
        block_copy(far, 0).wait()
    lax.fori_loop(1, owners // OUTER, wait_blocks, 0)
    own.wait()


def student_kernel(owners, most, codes_ref, recv_ref, cols_ref, learner_ref, grad_ref, loss_ref, target_ref):
    me = lax.axis_index("vocab")
    row_count, width = learner_ref.shape
    half = row_count // 2
    sb_local = width // BLK
    vocab_width = float(width * owners)

    def clear(c, carry):
        target_ref[c] = jnp.zeros((half, LANES), jnp.float32)
        return carry

    lax.fori_loop(0, sb_local, clear, 0)
    low = low_lanes((half, LANES))
    for source in range(owners):
        column = cols_ref[:, source:source + 1]
        scale = jnp.where(low, column[:half], column[half:])
        for at in range(most):
            code = codes_ref[source, me * most + at].astype(jnp.int32)
            block = jnp.where(code < 0, sb_local, code)
            target_ref[block] = target_ref[block] + recv_ref[source, at].astype(jnp.float32) * scale

    target_total = cols_ref[:, owners:owners + 1] * vocab_width
    lse = cols_ref[:, owners + 1:owners + 2]

    def pair(j, loss):
        first, second = target_ref[2 * j], target_ref[2 * j + 1]
        target = jnp.concatenate([
            jnp.where(low, first, pltpu.roll(second, BLK, 1)),
            jnp.where(low, pltpu.roll(first, BLK, 1), second),
        ], axis=0)
        at = pl.ds(pl.multiple_of(j * LANES, LANES), LANES)
        logprob = learner_ref[:, at].astype(jnp.float32) / float(SMOOTHING_HEAT) - lse
        grad_ref[:, at] = (target_total * jnp.exp(logprob) - vocab_width * target).astype(jnp.bfloat16)
        fed = target > 0.0
        return loss + jnp.where(fed, target * (jnp.log(jnp.where(fed, target, 1.0)) - logprob), 0.0)

    loss = lax.fori_loop(0, sb_local // 2, pair, jnp.zeros((row_count, LANES), jnp.float32))
    loss_ref[...] = jnp.sum(loss.reshape(row_count // 8, 8, LANES), axis=0)


def loss_kernel(parts, owners, scale, loss_ref, result_ref, table, send, recv):
    me = lax.axis_index("dp") * owners + lax.axis_index("vocab")
    everyone = parts * owners

    def device(k):
        peer = lax.rem(me + k, everyone)
        return (peer // owners, lax.rem(peer, owners))

    barrier = pltpu.get_barrier_semaphore()

    def greet(k, carry):
        pl.semaphore_signal(barrier, inc=1, device_id=device(k), device_id_type=MESH)
        return carry

    lax.fori_loop(1, everyone, greet, 0)
    table[me] = loss_ref[...]
    pl.semaphore_wait(barrier, everyone - 1)

    def copy(k):
        return pltpu.make_async_remote_copy(
            src_ref=loss_ref, dst_ref=table.at[me], send_sem=send.at[k], recv_sem=recv.at[k],
            device_id=device(k), device_id_type=MESH)

    def start(k, carry):
        copy(k).start()
        return carry

    def wait(k, carry):
        copy(k).wait()
        return carry

    lax.fori_loop(1, everyone, start, 0)
    lax.fori_loop(1, everyone, wait, 0)
    total = jnp.sum(table[...], axis=0)
    total = jnp.sum(jnp.sum(total, axis=0, keepdims=True), axis=1, keepdims=True)
    result_ref[...] = total * scale


def per_device(mentor_score_matrix, learner_score_matrix, align_dev, align_slot, align_weight):
    parts, owners = lax.axis_size("dp"), lax.axis_size("vocab")
    row_count, _ = mentor_score_matrix.shape
    half = row_count // 2
    tb_local, topk = align_dev.shape
    most = max(2, 3 * tb_local * topk // (2 * owners))
    width = learner_score_matrix.shape[1]
    sb_local = width // BLK
    vmem = pl.BlockSpec(memory_space=pltpu.VMEM)
    smem = pl.BlockSpec(memory_space=pltpu.SMEM)
    anywhere = pl.BlockSpec(memory_space=pl.ANY)

    weight = align_weight.reshape(tb_local * topk, BLK, BLK)
    weight = jnp.concatenate([weight, weight], axis=2)

    outgoing, stats = pl.pallas_call(
        functools.partial(teacher_kernel, owners, most),
        out_shape=(
            jax.ShapeDtypeStruct((owners * most, half, LANES), jnp.bfloat16),
            jax.ShapeDtypeStruct((STATS, row_count), jnp.float32),
        ),
        in_specs=[smem, smem, vmem, vmem],
        out_specs=(vmem, vmem),
        scratch_shapes=[pltpu.SMEM((owners,), jnp.int32), pltpu.SMEM((tb_local * topk,), jnp.int32)],
        compiler_params=pltpu.CompilerParams(vmem_limit_bytes=VMEM_BYTES),
        name="teacher_terms",
    )(align_dev.T, align_slot.T, mentor_score_matrix, weight)

    arrived, columns, codes = pl.pallas_call(
        functools.partial(exchange_kernel, owners),
        out_shape=(
            jax.ShapeDtypeStruct((owners, most, half, LANES), jnp.bfloat16),
            jax.ShapeDtypeStruct((row_count, LANES), jnp.float32),
            jax.ShapeDtypeStruct((owners, row_count), jnp.float32),
        ),
        in_specs=[vmem, vmem, anywhere],
        out_specs=(anywhere, vmem, vmem),
        scratch_shapes=[
            pltpu.VMEM((row_count, width), jnp.bfloat16),
            pltpu.VMEM((STATS, row_count), jnp.float32),
            pltpu.VMEM((owners, STATS, row_count), jnp.float32),
            pltpu.SemaphoreType.DMA((owners,)),
            pltpu.SemaphoreType.DMA((owners,)),
            pltpu.SemaphoreType.DMA((owners,)),
            pltpu.SemaphoreType.DMA((owners,)),
            pltpu.SemaphoreType.DMA((2,)),
        ],
        compiler_params=pltpu.CompilerParams(
            collective_id=0, has_side_effects=True, vmem_limit_bytes=VMEM_BYTES),
        name="exchange",
    )(outgoing.reshape(owners, most, half, LANES), stats, learner_score_matrix)

    scaled_grad, loss = pl.pallas_call(
        functools.partial(student_kernel, owners, most),
        out_shape=(
            jax.ShapeDtypeStruct((row_count, width), jnp.bfloat16),
            jax.ShapeDtypeStruct((8, LANES), jnp.float32),
        ),
        in_specs=[smem, vmem, vmem, vmem],
        out_specs=(vmem, vmem),
        scratch_shapes=[pltpu.VMEM((sb_local + 1, half, LANES), jnp.float32)],
        compiler_params=pltpu.CompilerParams(vmem_limit_bytes=VMEM_BYTES),
        name="student_gradient",
    )(codes, arrived, columns, learner_score_matrix)

    scale = float(SMOOTHING_HEAT) * float(SMOOTHING_HEAT) / float(row_count * parts)
    total = pl.pallas_call(
        functools.partial(loss_kernel, parts, owners, scale),
        out_shape=jax.ShapeDtypeStruct((1, 1), jnp.float32),
        in_specs=[vmem],
        out_specs=vmem,
        scratch_shapes=[
            pltpu.VMEM((parts * owners, 8, LANES), jnp.float32),
            pltpu.SemaphoreType.DMA((parts * owners,)),
            pltpu.SemaphoreType.DMA((parts * owners,)),
        ],
        compiler_params=pltpu.CompilerParams(collective_id=1, has_side_effects=True),
        name="loss_sum",
    )(loss)
    return scaled_grad, total[0, 0]


def solution(mesh):
    in_specs = (
        P("dp", "vocab"),
        P("dp", "vocab"),
        P("vocab", None),
        P("vocab", None),
        P("vocab", None, None),
    )
    out_specs = (P("dp", "vocab"), P())
    return jax.shard_map(
        per_device, mesh=mesh, in_specs=in_specs, out_specs=out_specs, check_vma=False
    )
```

```python
import functools

import jax
import jax.numpy as jnp
from jax import lax
from jax.experimental import pallas as pl
from jax.experimental.pallas import tpu as pltpu
from jax.sharding import PartitionSpec as P

BLK = 64
SMOOTHING_HEAT = 2
LANES = 128
STATS = 8
OUTER = 4
FAR = (0, 2, 1, 3)
VMEM_BYTES = 24 * 1024 * 1024
MESH = pl.DeviceIdType.MESH


def low_lanes(shape):
    return lax.broadcasted_iota(jnp.int32, shape, len(shape) - 1) < BLK


def columns_to_rows(columns, first, count):
    rows = columns[0].shape[0]
    lane = lax.broadcasted_iota(jnp.int32, (rows, LANES), 1)
    table = jnp.zeros((rows, LANES), jnp.float32)
    for at, column in enumerate(columns):
        table = jnp.where(lane == first + at, column, table)
    return jnp.transpose(table)[:count]


def teacher_kernel(owners, most, dev_ref, slot_ref, mentor_ref, weight_ref, out_ref, stats_ref, codes_ref, count_ref, place_ref):
    row_count, width = mentor_ref.shape
    half = row_count // 2
    topk = dev_ref.shape[0]
    tb_local = dev_ref.shape[1]

    for owner in range(owners):
        count_ref[owner] = 0
    code_lane = lax.broadcasted_iota(jnp.int32, (8, LANES), 1)

    def place(b, codes):
        for k in range(topk):
            owner = dev_ref[k, b]
            earlier = count_ref[owner]
            count_ref[owner] = earlier + 1
            position = owner * most + earlier
            place_ref[b * topk + k] = position
            codes = jnp.where(code_lane == position, slot_ref[k, b], codes)
        return codes

    codes_ref[...] = lax.fori_loop(0, tb_local, place, jnp.full((8, LANES), -1, jnp.int32))

    tiles = width // LANES
    high = mentor_ref[:, :LANES]
    for tile in range(1, tiles):
        high = jnp.maximum(high, mentor_ref[:, tile * LANES:(tile + 1) * LANES])
    high = jnp.max(high.astype(jnp.float32), axis=1, keepdims=True) / float(SMOOTHING_HEAT)

    low = low_lanes((BLK, LANES))
    none = jnp.zeros((BLK, LANES), jnp.bfloat16)

    def pair(j, carry):
        total, mass = carry
        x = mentor_ref[:, pl.ds(pl.multiple_of(j * LANES, LANES), LANES)].astype(jnp.float32)
        e = jnp.exp(x / float(SMOOTHING_HEAT) - high)
        total = total + e
        e = e.astype(jnp.bfloat16)
        lhs = jnp.concatenate([e[:half], e[half:]], axis=1)
        lefts, rights = [], []
        for b in range(2):
            blocks = [weight_ref[(2 * j + b) * topk + k] for k in range(topk)]
            pad_before, pad_after = [none] * (topk * b), [none] * (topk * (1 - b))
            lefts.append(jnp.concatenate(pad_before + [jnp.where(low, w, none) for w in blocks] + pad_after, axis=1))
            rights.append(jnp.concatenate(pad_before + [jnp.where(low, none, w) for w in blocks] + pad_after, axis=1))
        rhs = jnp.concatenate(lefts + rights, axis=0)
        terms = jnp.dot(lhs, rhs, preferred_element_type=jnp.float32).astype(jnp.bfloat16)
        for at in range(2 * topk):
            term = terms[:, at * LANES:(at + 1) * LANES]
            out_ref[place_ref[2 * topk * j + at]] = term
            mass = mass + term.astype(jnp.float32)
        return total, mass

    total, mass = lax.fori_loop(
        0, tiles, pair,
        (jnp.zeros((row_count, LANES), jnp.float32), jnp.zeros((half, LANES), jnp.float32)),
    )
    low = low_lanes((half, LANES))
    mass = jnp.concatenate([
        jnp.sum(jnp.where(low, mass, 0.0), axis=1, keepdims=True),
        jnp.sum(jnp.where(low, 0.0, mass), axis=1, keepdims=True),
    ], axis=0)
    total = jnp.sum(total, axis=1, keepdims=True)
    stats_ref[...] = columns_to_rows([high, total, mass], 0, STATS)


def outer_partner(outer, far):
    return (outer, outer + 1 - 2 * lax.rem(outer, 2), lax.rem(outer + 2, OUTER), OUTER - 1 - outer)[far]


def student_kernel(parts, owners, most, loss_scale,
                   out_ref, stats_ref, codes_ref, learner_ref, grad_ref, loss_ref,
                   received, sums, scale, message, teacher_table, student_table, code_table, code_smem,
                   history, history_smem, part_loss, part_table, loss_message, loss_table,
                   send, recv, local):
    dp, me = lax.axis_index("dp"), lax.axis_index("vocab")
    row_count, width = learner_ref.shape
    half = row_count // 2
    tiles = width // LANES
    slots = owners * most
    inner = owners // OUTER
    vocab_width = float(width * owners)
    low = low_lanes((half, LANES))

    def partner(near, order):
        return outer_partner(me // inner, FAR[order]) * inner + lax.rem(lax.rem(me, inner) + near, inner)

    def copy_to(kind, near, order, src, dst):
        peer = partner(near, order)
        slot = near * OUTER + order
        return pltpu.make_async_remote_copy(
            src_ref=out_ref.at[peer] if src is None else src, dst_ref=dst.at[slot],
            send_sem=send.at[kind, slot], recv_sem=recv.at[kind, slot],
            device_id=(dp, peer), device_id_type=MESH)

    def blocks(near, order):
        return copy_to(0, near, order, None, received)

    def teacher_stats(near, order):
        return copy_to(1, near, order, stats_ref, teacher_table)

    def slot_codes(near, order):
        return copy_to(2, near, order, codes_ref, code_table)

    def student_stats(near, order):
        return copy_to(3, near, order, message, student_table)

    def losses(near, order):
        return copy_to(4, near, order, loss_message, loss_table)

    def each(action):
        for order in range(1, OUTER):
            action(0, order)
        rest(action)

    def rest(action):
        def body(near, carry):
            for order in range(OUTER):
                action(near, order)
            return carry

        lax.fori_loop(1, inner, body, 0)

    def part_copy(k):
        return pltpu.make_async_remote_copy(
            src_ref=part_loss, dst_ref=part_table.at[dp], send_sem=send.at[5, k], recv_sem=recv.at[5, k],
            device_id=(lax.rem(dp + k, parts), me), device_id_type=MESH)

    barrier = pltpu.get_barrier_semaphore()

    def greet(near, order):
        pl.semaphore_signal(barrier, inc=1, device_id=(dp, partner(near, order)), device_id_type=MESH)

    each(greet)
    for k in range(1, parts):
        pl.semaphore_signal(barrier, inc=1, device_id=(lax.rem(dp + k, parts), me), device_id_type=MESH)
    pl.semaphore_wait(barrier, owners + parts - 2)

    for order in range(1, OUTER):
        blocks(0, order).start()

    def start_small(near, order):
        slot_codes(near, order).start()
        teacher_stats(near, order).start()

    each(start_small)
    rest(lambda near, order: blocks(near, order).start())

    teacher_table[0] = stats_ref[...]
    code_table[0] = codes_ref[...]

    def tile_of(j):
        return learner_ref[:, pl.ds(pl.multiple_of(j * LANES, LANES), LANES)]

    high = lax.fori_loop(1, tiles, lambda j, h: jnp.maximum(h, tile_of(j)), learner_ref[:, :LANES])
    high = jnp.max(high.astype(jnp.float32), axis=1, keepdims=True) / float(SMOOTHING_HEAT)

    def add_exp(j, total):
        return total + jnp.exp(tile_of(j).astype(jnp.float32) / float(SMOOTHING_HEAT) - high)

    total = lax.fori_loop(0, tiles, add_exp, jnp.zeros((row_count, LANES), jnp.float32))
    total = jnp.sum(total, axis=1, keepdims=True)
    message[...] = columns_to_rows([high, total], 0, STATS)
    student_table[0] = message[...]
    each(lambda near, order: student_stats(near, order).start())

    each(lambda near, order: slot_codes(near, order).wait())
    fetch = pltpu.make_async_copy(code_table, code_smem, local.at[0])
    fetch.start()
    fetch.wait()
    lane = lax.broadcasted_iota(jnp.int32, (1, LANES), 1)

    def note(q, last):
        history[pl.ds(q, 1), :] = last
        code = code_smem[q // most, 0, me * most + lax.rem(q, most)]
        return jnp.where(lane == code, q, last)

    last = lax.fori_loop(0, slots, note, jnp.full((1, LANES), slots, jnp.int32))
    history[pl.ds(slots, 1), :] = last
    fetch = pltpu.make_async_copy(history, history_smem, local.at[1])
    fetch.start()
    sums[slots] = jnp.zeros((half, LANES), jnp.float32)

    each(lambda near, order: teacher_stats(near, order).wait())
    teacher_high = teacher_table[:, 0, :]
    teacher_scale = jnp.exp(teacher_high - jnp.max(teacher_high, axis=0, keepdims=True))
    weight = teacher_scale / jnp.sum(teacher_table[:, 1, :] * teacher_scale, axis=0, keepdims=True)
    target_total = jnp.sum(teacher_table[:, 2, :] * weight, axis=0, keepdims=True)
    fill = jnp.zeros((LANES - owners - 1, row_count), jnp.float32)
    columns = jnp.transpose(jnp.concatenate([weight, target_total, fill], axis=0))
    for source in range(owners):
        column = columns[:, source:source + 1]
        scale[source] = jnp.where(low, column[:half], column[half:])
    target_total = columns[:, owners:owners + 1] * vocab_width
    fetch.wait()

    def add_blocks(slot, source_ref, index):
        for at in range(most):
            q = slot * most + at
            code = code_smem[slot, 0, me * most + at]
            earlier = sums[history_smem[q, jnp.maximum(code, 0)]]
            sums[q] = earlier + source_ref[index, at].astype(jnp.float32) * scale[slot]

    add_blocks(0, out_ref, me)

    def take(near, order):
        blocks(near, order).wait()
        slot = near * OUTER + order
        add_blocks(slot, received, slot)

    each(take)

    each(lambda near, order: student_stats(near, order).wait())
    student_high = student_table[:, 0, :]
    top = jnp.max(student_high, axis=0, keepdims=True)
    lse = top + jnp.log(jnp.sum(student_table[:, 1, :] * jnp.exp(student_high - top), axis=0, keepdims=True))
    lse = jnp.transpose(jnp.concatenate([lse, jnp.zeros((LANES - 1, row_count), jnp.float32)], axis=0))[:, :1]

    def pair(j, loss):
        first = sums[history_smem[slots, 2 * j]]
        second = sums[history_smem[slots, 2 * j + 1]]
        target = jnp.concatenate([
            jnp.where(low, first, pltpu.roll(second, BLK, 1)),
            jnp.where(low, pltpu.roll(first, BLK, 1), second),
        ], axis=0)
        at = pl.ds(pl.multiple_of(j * LANES, LANES), LANES)
        logprob = learner_ref[:, at].astype(jnp.float32) / float(SMOOTHING_HEAT) - lse
        grad_ref[:, at] = (target_total * jnp.exp(logprob) - vocab_width * target).astype(jnp.bfloat16)
        return loss + jnp.where(target > 0.0, target * (jnp.log(target) - logprob), 0.0)

    loss = lax.fori_loop(0, tiles, pair, jnp.zeros((row_count, LANES), jnp.float32))
    loss = jnp.sum(loss.reshape(row_count // 8, 8, LANES), axis=0)
    part_loss[...] = loss
    for k in range(1, parts):
        part_copy(k).start()
    part_table[dp] = loss
    for k in range(1, parts):
        part_copy(k).wait()
    loss = jnp.sum(part_table[...], axis=0)
    loss_message[...] = loss
    each(lambda near, order: losses(near, order).start())
    loss_table[0] = loss
    each(lambda near, order: losses(near, order).wait())
    totals = jnp.sum(jnp.sum(loss_table[...], axis=1), axis=1, keepdims=True)
    loss_ref[...] = jnp.sum(totals, axis=0, keepdims=True) * loss_scale


def per_device(mentor_score_matrix, learner_score_matrix, align_dev, align_slot, align_weight):
    parts, owners = lax.axis_size("dp"), lax.axis_size("vocab")
    row_count, _ = mentor_score_matrix.shape
    half = row_count // 2
    tb_local, topk = align_dev.shape
    most = max(2, 3 * tb_local * topk // (2 * owners))
    width = learner_score_matrix.shape[1]
    vmem = pl.BlockSpec(memory_space=pltpu.VMEM)
    smem = pl.BlockSpec(memory_space=pltpu.SMEM)

    weight = align_weight.reshape(tb_local * topk, BLK, BLK)
    weight = jnp.concatenate([weight, weight], axis=2)

    outgoing, stats, codes = pl.pallas_call(
        functools.partial(teacher_kernel, owners, most),
        out_shape=(
            jax.ShapeDtypeStruct((owners * most, half, LANES), jnp.bfloat16),
            jax.ShapeDtypeStruct((STATS, row_count), jnp.float32),
            jax.ShapeDtypeStruct((8, LANES), jnp.int32),
        ),
        in_specs=[smem, smem, vmem, vmem],
        out_specs=(vmem, vmem, vmem),
        scratch_shapes=[pltpu.SMEM((owners,), jnp.int32), pltpu.SMEM((tb_local * topk,), jnp.int32)],
        compiler_params=pltpu.CompilerParams(vmem_limit_bytes=VMEM_BYTES),
        name="teacher_terms",
    )(align_dev.T, align_slot.T, mentor_score_matrix, weight)

    loss_scale = float(SMOOTHING_HEAT) * float(SMOOTHING_HEAT) / float(row_count * parts)
    slots = owners * most
    history_rows = (slots // 8 + 1) * 8
    small = pltpu.VMEM((8, LANES), jnp.float32)
    scaled_grad, loss = pl.pallas_call(
        functools.partial(student_kernel, parts, owners, most, loss_scale),
        out_shape=(
            jax.ShapeDtypeStruct((row_count, width), jnp.bfloat16),
            jax.ShapeDtypeStruct((1, 1), jnp.float32),
        ),
        in_specs=[vmem, vmem, vmem, vmem],
        out_specs=(vmem, vmem),
        scratch_shapes=[
            pltpu.VMEM((owners, most, half, LANES), jnp.bfloat16),
            pltpu.VMEM((slots + 1, half, LANES), jnp.float32),
            pltpu.VMEM((owners, half, LANES), jnp.float32),
            pltpu.VMEM((STATS, row_count), jnp.float32),
            pltpu.VMEM((owners, STATS, row_count), jnp.float32),
            pltpu.VMEM((owners, STATS, row_count), jnp.float32),
            pltpu.VMEM((owners, 8, LANES), jnp.int32),
            pltpu.SMEM((owners, 8, LANES), jnp.int32),
            pltpu.VMEM((history_rows, LANES), jnp.int32),
            pltpu.SMEM((history_rows, LANES), jnp.int32),
            small,
            pltpu.VMEM((parts, 8, LANES), jnp.float32),
            small,
            pltpu.VMEM((owners, 8, LANES), jnp.float32),
            pltpu.SemaphoreType.DMA((6, owners)),
            pltpu.SemaphoreType.DMA((6, owners)),
            pltpu.SemaphoreType.DMA((2,)),
        ],
        compiler_params=pltpu.CompilerParams(
            collective_id=0, has_side_effects=True, vmem_limit_bytes=VMEM_BYTES),
        name="exchange_and_gradient",
    )(outgoing.reshape(owners, most, half, LANES), stats, codes, learner_score_matrix)
    return scaled_grad, loss[0, 0]


def solution(mesh):
    in_specs = (
        P("dp", "vocab"),
        P("dp", "vocab"),
        P("vocab", None),
        P("vocab", None),
        P("vocab", None, None),
    )
    out_specs = (P("dp", "vocab"), P())
    return jax.shard_map(
        per_device, mesh=mesh, in_specs=in_specs, out_specs=out_specs, check_vma=False
    )
```

```python
import functools

import jax
import jax.numpy as jnp
from jax import lax
from jax.experimental import pallas as pl
from jax.experimental.pallas import tpu as pltpu
from jax.sharding import PartitionSpec as P

BLK = 64
SMOOTHING_HEAT = 2
LANES = 128
CHUNKS = 2
TEACHER_STATS = 3
STUDENT_STATS = 2
OUTER = 4
FAR = (0, 2, 1, 3)
VMEM_BYTES = 24 * 1024 * 1024
MESH = pl.DeviceIdType.MESH


def low_lanes(shape):
    return lax.broadcasted_iota(jnp.int32, shape, len(shape) - 1) < BLK


def columns_to_row(columns, row_ref):
    rows = columns[0].shape[0]
    lane = lax.broadcasted_iota(jnp.int32, (rows, LANES), 1)
    table = jnp.zeros((rows, LANES), jnp.float32)
    for at, column in enumerate(columns):
        table = jnp.where(lane == at, column, table)
    table = jnp.transpose(table)
    for at in range(len(columns)):
        row_ref[:, at * rows:(at + 1) * rows] = table[at:at + 1]


def teacher_kernel(owners, most, dev_ref, slot_ref, mentor_ref, weight_ref, out_ref, stats_ref, codes_ref, count_ref, place_ref):
    row_count, width = mentor_ref.shape
    half = row_count // 2
    rows = half // CHUNKS
    topk = dev_ref.shape[0]
    tb_local = dev_ref.shape[1]

    for owner in range(owners):
        count_ref[owner] = 0
    code_lane = lax.broadcasted_iota(jnp.int32, (1, LANES), 1)

    def place(b, codes):
        for k in range(topk):
            owner = dev_ref[k, b]
            earlier = count_ref[owner]
            count_ref[owner] = earlier + 1
            position = owner * most + earlier
            place_ref[b * topk + k] = position
            codes = jnp.where(code_lane == position, slot_ref[k, b], codes)
        return codes

    codes_ref[...] = lax.fori_loop(0, tb_local, place, jnp.full((1, LANES), -1, jnp.int32))

    tiles = width // LANES
    high = mentor_ref[:, :LANES]
    for tile in range(1, tiles):
        high = jnp.maximum(high, mentor_ref[:, tile * LANES:(tile + 1) * LANES])
    high = jnp.max(high.astype(jnp.float32), axis=1, keepdims=True) / float(SMOOTHING_HEAT)

    low = low_lanes((BLK, LANES))
    none = jnp.zeros((BLK, LANES), jnp.bfloat16)

    def pair(j, carry):
        total, mass = carry
        x = mentor_ref[:, pl.ds(pl.multiple_of(j * LANES, LANES), LANES)].astype(jnp.float32)
        e = jnp.exp(x / float(SMOOTHING_HEAT) - high)
        total = total + e
        e = e.astype(jnp.bfloat16)
        lhs = jnp.concatenate([e[:half], e[half:]], axis=1)
        lefts, rights = [], []
        for b in range(2):
            blocks = [weight_ref[(2 * j + b) * topk + k] for k in range(topk)]
            pad_before, pad_after = [none] * (topk * b), [none] * (topk * (1 - b))
            lefts.append(jnp.concatenate(pad_before + [jnp.where(low, w, none) for w in blocks] + pad_after, axis=1))
            rights.append(jnp.concatenate(pad_before + [jnp.where(low, none, w) for w in blocks] + pad_after, axis=1))
        rhs = jnp.concatenate(lefts + rights, axis=0)
        terms = jnp.dot(lhs, rhs, preferred_element_type=jnp.float32).astype(jnp.bfloat16)
        for at in range(2 * topk):
            term = terms[:, at * LANES:(at + 1) * LANES]
            for chunk in range(CHUNKS):
                out_ref[chunk, place_ref[2 * topk * j + at]] = term[chunk * rows:(chunk + 1) * rows]
            mass = mass + term.astype(jnp.float32)
        return total, mass

    total, mass = lax.fori_loop(
        0, tiles, pair,
        (jnp.zeros((row_count, LANES), jnp.float32), jnp.zeros((half, LANES), jnp.float32)),
    )
    low = low_lanes((half, LANES))
    mass = jnp.concatenate([
        jnp.sum(jnp.where(low, mass, 0.0), axis=1, keepdims=True),
        jnp.sum(jnp.where(low, 0.0, mass), axis=1, keepdims=True),
    ], axis=0)
    total = jnp.sum(total, axis=1, keepdims=True)
    columns_to_row([high, total, mass], stats_ref)


def outer_partner(outer, far):
    return (outer, outer + 1 - 2 * lax.rem(outer, 2), lax.rem(outer + 2, OUTER), OUTER - 1 - outer)[far]


def student_kernel(parts, owners, most, loss_scale,
                   out_ref, stats_ref, codes_ref, learner_ref, grad_ref, loss_ref,
                   received, sums, scale, message, teacher_table, student_table, code_table, code_smem,
                   history, history_smem, part_loss, part_table, loss_message, loss_table,
                   send, recv, local):
    dp, me = lax.axis_index("dp"), lax.axis_index("vocab")
    row_count, width = learner_ref.shape
    half = row_count // 2
    rows = half // CHUNKS
    tiles = width // LANES
    slots = owners * most
    inner = owners // OUTER
    vocab_width = float(width * owners)
    low = low_lanes((half, LANES))
    low_rows = low_lanes((rows, LANES))

    def partner(near, order):
        return outer_partner(me // inner, FAR[order]) * inner + lax.rem(lax.rem(me, inner) + near, inner)

    def copy_to(kind, near, order, src, dst):
        slot = near * OUTER + order
        return pltpu.make_async_remote_copy(
            src_ref=src, dst_ref=dst.at[slot], send_sem=send.at[kind, slot], recv_sem=recv.at[kind, slot],
            device_id=(dp, partner(near, order)), device_id_type=MESH)

    def blocks(chunk, near, order):
        return copy_to(chunk, near, order, out_ref.at[chunk, partner(near, order)], received.at[chunk])

    def teacher_stats(near, order):
        return copy_to(CHUNKS, near, order, stats_ref, teacher_table)

    def slot_codes(near, order):
        return copy_to(CHUNKS + 1, near, order, codes_ref, code_table)

    def student_stats(near, order):
        return copy_to(CHUNKS + 2, near, order, message, student_table)

    def losses(near, order):
        return copy_to(CHUNKS + 3, near, order, loss_message, loss_table)

    def each(action):
        for order in range(1, OUTER):
            action(0, order)
        rest(action)

    def rest(action):
        def body(near, carry):
            for order in range(OUTER):
                action(near, order)
            return carry

        lax.fori_loop(1, inner, body, 0)

    def part_copy(k):
        return pltpu.make_async_remote_copy(
            src_ref=part_loss, dst_ref=part_table.at[dp], send_sem=send.at[CHUNKS + 4, k], recv_sem=recv.at[CHUNKS + 4, k],
            device_id=(lax.rem(dp + k, parts), me), device_id_type=MESH)

    barrier = pltpu.get_barrier_semaphore()

    def greet(near, order):
        pl.semaphore_signal(barrier, inc=1, device_id=(dp, partner(near, order)), device_id_type=MESH)

    each(greet)
    for k in range(1, parts):
        pl.semaphore_signal(barrier, inc=1, device_id=(lax.rem(dp + k, parts), me), device_id_type=MESH)
    pl.semaphore_wait(barrier, owners + parts - 2)

    for order in range(1, OUTER):
        blocks(0, 0, order).start()

    def start_small(near, order):
        slot_codes(near, order).start()
        teacher_stats(near, order).start()

    each(start_small)
    rest(lambda near, order: blocks(0, near, order).start())

    teacher_table[0] = stats_ref[...]
    code_table[0] = codes_ref[...]

    def tile_of(j):
        return learner_ref[:, pl.ds(pl.multiple_of(j * LANES, LANES), LANES)]

    high = lax.fori_loop(1, tiles, lambda j, h: jnp.maximum(h, tile_of(j)), learner_ref[:, :LANES])
    high = jnp.max(high.astype(jnp.float32), axis=1, keepdims=True) / float(SMOOTHING_HEAT)

    def add_exp(j, total):
        return total + jnp.exp(tile_of(j).astype(jnp.float32) / float(SMOOTHING_HEAT) - high)

    total = lax.fori_loop(0, tiles, add_exp, jnp.zeros((row_count, LANES), jnp.float32))
    total = jnp.sum(total, axis=1, keepdims=True)
    columns_to_row([high, total], message)
    student_table[0] = message[...]
    each(lambda near, order: student_stats(near, order).start())
    for chunk in range(1, CHUNKS):
        each(lambda near, order: blocks(chunk, near, order).start())

    each(lambda near, order: slot_codes(near, order).wait())
    fetch = pltpu.make_async_copy(code_table, code_smem, local.at[0])
    fetch.start()
    fetch.wait()
    lane = lax.broadcasted_iota(jnp.int32, (1, LANES), 1)

    def note(q, last):
        history[pl.ds(q, 1), :] = last
        code = code_smem[q // most, 0, me * most + lax.rem(q, most)]
        return jnp.where(lane == code, q, last)

    last = lax.fori_loop(0, slots, note, jnp.full((1, LANES), slots, jnp.int32))
    history[pl.ds(slots, 1), :] = last
    fetch = pltpu.make_async_copy(history, history_smem, local.at[1])
    fetch.start()
    for chunk in range(CHUNKS):
        sums[chunk, slots] = jnp.zeros((rows, LANES), jnp.float32)

    each(lambda near, order: teacher_stats(near, order).wait())
    teacher_high, teacher_sum, teacher_mass = (
        teacher_table[:, 0, at * row_count:(at + 1) * row_count] for at in range(TEACHER_STATS))
    teacher_scale = jnp.exp(teacher_high - jnp.max(teacher_high, axis=0, keepdims=True))
    weight = teacher_scale / jnp.sum(teacher_sum * teacher_scale, axis=0, keepdims=True)
    target_total = jnp.sum(teacher_mass * weight, axis=0, keepdims=True)
    fill = jnp.zeros((LANES - owners - 1, row_count), jnp.float32)
    columns = jnp.transpose(jnp.concatenate([weight, target_total, fill], axis=0))
    for source in range(owners):
        column = columns[:, source:source + 1]
        scale[source] = jnp.where(low, column[:half], column[half:])
    target_total = columns[:, owners:owners + 1] * vocab_width
    fetch.wait()

    def add_blocks(chunk, slot, source_ref, index):
        at_rows = pl.ds(chunk * rows, rows)
        for at in range(most):
            q = slot * most + at
            code = code_smem[slot, 0, me * most + at]
            earlier = sums[chunk, history_smem[q, jnp.maximum(code, 0)]]
            sums[chunk, q] = earlier + source_ref[chunk, index, at].astype(jnp.float32) * scale[slot, at_rows, :]

    def gather(chunk):
        add_blocks(chunk, 0, out_ref, me)

        def take(near, order):
            blocks(chunk, near, order).wait()
            slot = near * OUTER + order
            add_blocks(chunk, slot, received, slot)

        each(take)

    def chunk_rows(chunk, column):
        top = chunk * rows
        return jnp.concatenate([column[top:top + rows], column[half + top:half + top + rows]], axis=0)

    def tile(chunk, j):
        first = sums[chunk, history_smem[slots, 2 * j]]
        second = sums[chunk, history_smem[slots, 2 * j + 1]]
        target = jnp.concatenate([
            jnp.where(low_rows, first, pltpu.roll(second, BLK, 1)),
            jnp.where(low_rows, pltpu.roll(first, BLK, 1), second),
        ], axis=0)
        at = pl.ds(pl.multiple_of(j * LANES, LANES), LANES)
        top = pl.ds(chunk * rows, rows)
        bottom = pl.ds(half + chunk * rows, rows)
        logits = jnp.concatenate([learner_ref[top, at], learner_ref[bottom, at]], axis=0).astype(jnp.float32)
        return target, logits / float(SMOOTHING_HEAT), at, top, bottom

    def add_loss(chunk, loss):
        lse_rows = chunk_rows(chunk, lse)

        def body(j, loss):
            target, logits, _, _, _ = tile(chunk, j)
            return loss + jnp.where(target > 0.0, target * (jnp.log(target) - (logits - lse_rows)), 0.0)

        return lax.fori_loop(0, tiles, body, loss)

    def write_gradient(chunk, first, end):
        lse_rows, total_rows = chunk_rows(chunk, lse), chunk_rows(chunk, target_total)

        def body(j, carry):
            target, logits, at, top, bottom = tile(chunk, j)
            grad = (total_rows * jnp.exp(logits - lse_rows) - vocab_width * target).astype(jnp.bfloat16)
            grad_ref[top, at] = grad[:rows]
            grad_ref[bottom, at] = grad[rows:]
            return carry

        lax.fori_loop(first, end, body, 0)

    gather(0)
    each(lambda near, order: student_stats(near, order).wait())
    student_high, student_sum = (
        student_table[:, 0, at * row_count:(at + 1) * row_count] for at in range(STUDENT_STATS))
    top = jnp.max(student_high, axis=0, keepdims=True)
    lse = top + jnp.log(jnp.sum(student_sum * jnp.exp(student_high - top), axis=0, keepdims=True))
    lse = jnp.transpose(jnp.concatenate([lse, jnp.zeros((LANES - 1, row_count), jnp.float32)], axis=0))[:, :1]

    loss = jnp.zeros((2 * rows, LANES), jnp.float32)
    for chunk in range(CHUNKS):
        if chunk:
            gather(chunk)
        loss = add_loss(chunk, loss)
        if chunk < CHUNKS - 1:
            write_gradient(chunk, 0, tiles)

    loss = jnp.sum(loss.reshape(2 * rows // 8, 8, LANES), axis=0)
    part_loss[...] = loss
    for k in range(1, parts):
        part_copy(k).start()
    part_table[dp] = loss
    write_gradient(CHUNKS - 1, 0, tiles // 2)
    for k in range(1, parts):
        part_copy(k).wait()
    loss = jnp.sum(part_table[...], axis=0)
    loss_message[...] = loss
    each(lambda near, order: losses(near, order).start())
    loss_table[0] = loss
    write_gradient(CHUNKS - 1, tiles // 2, tiles)
    each(lambda near, order: losses(near, order).wait())
    totals = jnp.sum(jnp.sum(loss_table[...], axis=1), axis=1, keepdims=True)
    loss_ref[...] = jnp.sum(totals, axis=0, keepdims=True) * loss_scale


def per_device(mentor_score_matrix, learner_score_matrix, align_dev, align_slot, align_weight):
    parts, owners = lax.axis_size("dp"), lax.axis_size("vocab")
    row_count, _ = mentor_score_matrix.shape
    rows = row_count // (2 * CHUNKS)
    tb_local, topk = align_dev.shape
    most = max(2, 3 * tb_local * topk // (2 * owners))
    width = learner_score_matrix.shape[1]
    vmem = pl.BlockSpec(memory_space=pltpu.VMEM)
    smem = pl.BlockSpec(memory_space=pltpu.SMEM)

    weight = align_weight.reshape(tb_local * topk, BLK, BLK)
    weight = jnp.concatenate([weight, weight], axis=2)

    outgoing, stats, codes = pl.pallas_call(
        functools.partial(teacher_kernel, owners, most),
        out_shape=(
            jax.ShapeDtypeStruct((CHUNKS, owners * most, rows, LANES), jnp.bfloat16),
            jax.ShapeDtypeStruct((1, TEACHER_STATS * row_count), jnp.float32),
            jax.ShapeDtypeStruct((1, LANES), jnp.int32),
        ),
        in_specs=[smem, smem, vmem, vmem],
        out_specs=(vmem, vmem, vmem),
        scratch_shapes=[pltpu.SMEM((owners,), jnp.int32), pltpu.SMEM((tb_local * topk,), jnp.int32)],
        compiler_params=pltpu.CompilerParams(vmem_limit_bytes=VMEM_BYTES),
        name="teacher_terms",
    )(align_dev.T, align_slot.T, mentor_score_matrix, weight)

    loss_scale = float(SMOOTHING_HEAT) * float(SMOOTHING_HEAT) / float(row_count * parts)
    slots = owners * most
    history_rows = (slots // 8 + 1) * 8
    small = pltpu.VMEM((8, LANES), jnp.float32)
    scaled_grad, loss = pl.pallas_call(
        functools.partial(student_kernel, parts, owners, most, loss_scale),
        out_shape=(
            jax.ShapeDtypeStruct((row_count, width), jnp.bfloat16),
            jax.ShapeDtypeStruct((1, 1), jnp.float32),
        ),
        in_specs=[vmem, vmem, vmem, vmem],
        out_specs=(vmem, vmem),
        scratch_shapes=[
            pltpu.VMEM((CHUNKS, owners, most, rows, LANES), jnp.bfloat16),
            pltpu.VMEM((CHUNKS, slots + 1, rows, LANES), jnp.float32),
            pltpu.VMEM((owners, CHUNKS * rows, LANES), jnp.float32),
            pltpu.VMEM((1, STUDENT_STATS * row_count), jnp.float32),
            pltpu.VMEM((owners, 1, TEACHER_STATS * row_count), jnp.float32),
            pltpu.VMEM((owners, 1, STUDENT_STATS * row_count), jnp.float32),
            pltpu.VMEM((owners, 1, LANES), jnp.int32),
            pltpu.SMEM((owners, 1, LANES), jnp.int32),
            pltpu.VMEM((history_rows, LANES), jnp.int32),
            pltpu.SMEM((history_rows, LANES), jnp.int32),
            small,
            pltpu.VMEM((parts, 8, LANES), jnp.float32),
            small,
            pltpu.VMEM((owners, 8, LANES), jnp.float32),
            pltpu.SemaphoreType.DMA((CHUNKS + 5, owners)),
            pltpu.SemaphoreType.DMA((CHUNKS + 5, owners)),
            pltpu.SemaphoreType.DMA((2,)),
        ],
        compiler_params=pltpu.CompilerParams(
            collective_id=0, has_side_effects=True, vmem_limit_bytes=VMEM_BYTES),
        name="exchange_and_gradient",
    )(outgoing.reshape(CHUNKS, owners, most, rows, LANES), stats, codes, learner_score_matrix)
    return scaled_grad, loss[0, 0]


def solution(mesh):
    in_specs = (
        P("dp", "vocab"),
        P("dp", "vocab"),
        P("vocab", None),
        P("vocab", None),
        P("vocab", None, None),
    )
    out_specs = (P("dp", "vocab"), P())
    return jax.shard_map(
        per_device, mesh=mesh, in_specs=in_specs, out_specs=out_specs, check_vma=False
    )
```

```python
import functools

import jax
import jax.numpy as jnp
from jax import lax
from jax.experimental import pallas as pl
from jax.experimental.pallas import tpu as pltpu
from jax.sharding import PartitionSpec as P

BLK = 64
SMOOTHING_HEAT = 2
LANES = 128
CHUNKS = 2
TEACHER_STATS = 3
STUDENT_STATS = 2
OUTER = 4
FAR = (0, 2, 1, 3)
VMEM_BYTES = 24 * 1024 * 1024
MESH = pl.DeviceIdType.MESH


def low_lanes(shape):
    return lax.broadcasted_iota(jnp.int32, shape, len(shape) - 1) < BLK


def columns_to_row(columns, row_ref):
    rows = columns[0].shape[0]
    lane = lax.broadcasted_iota(jnp.int32, (rows, LANES), 1)
    table = jnp.zeros((rows, LANES), jnp.float32)
    for at, column in enumerate(columns):
        table = jnp.where(lane == at, column, table)
    table = jnp.transpose(table)
    for at in range(len(columns)):
        row_ref[:, at * rows:(at + 1) * rows] = table[at:at + 1]


def outer_partner(outer, far):
    return (outer, outer + 1 - 2 * lax.rem(outer, 2), lax.rem(outer + 2, OUTER), OUTER - 1 - outer)[far]


def student_kernel(parts, owners, most, loss_scale,
                   dev_ref, slot_ref, mentor_ref, weight_ref, learner_ref, grad_ref, loss_ref,
                   exps, masks, mass, edges, edges_smem, own_codes, own_codes_smem, out, stats,
                   received, sums, scale, message, teacher_table, student_table, code_table, code_smem,
                   history, history_smem, part_loss, part_table, loss_message, loss_table,
                   send, recv, local):
    dp, me = lax.axis_index("dp"), lax.axis_index("vocab")
    row_count, width = learner_ref.shape
    half = row_count // 2
    rows = half // CHUNKS
    tiles = width // LANES
    slots = owners * most
    inner = owners // OUTER
    vocab_width = float(width * owners)
    low = low_lanes((half, LANES))
    low_rows = low_lanes((rows, LANES))

    def partner(near, order):
        return outer_partner(me // inner, FAR[order]) * inner + lax.rem(lax.rem(me, inner) + near, inner)

    def copy_to(kind, near, order, src, dst):
        slot = near * OUTER + order
        return pltpu.make_async_remote_copy(
            src_ref=src, dst_ref=dst.at[slot], send_sem=send.at[kind, slot], recv_sem=recv.at[kind, slot],
            device_id=(dp, partner(near, order)), device_id_type=MESH)

    def blocks(chunk, near, order):
        return copy_to(chunk, near, order, out.at[chunk, near * OUTER + order], received.at[chunk])

    def teacher_stats(near, order):
        return copy_to(CHUNKS, near, order, stats, teacher_table)

    def slot_codes(near, order):
        return copy_to(CHUNKS + 1, near, order, own_codes, code_table)

    def student_stats(near, order):
        return copy_to(CHUNKS + 2, near, order, message, student_table)

    def losses(near, order):
        return copy_to(CHUNKS + 3, near, order, loss_message, loss_table)

    def each(action):
        for order in range(1, OUTER):
            action(0, order)
        rest(action)

    def rest(action):
        def body(near, carry):
            for order in range(OUTER):
                action(near, order)
            return carry

        lax.fori_loop(1, inner, body, 0)

    def part_copy(k):
        return pltpu.make_async_remote_copy(
            src_ref=part_loss, dst_ref=part_table.at[dp], send_sem=send.at[CHUNKS + 4, k], recv_sem=recv.at[CHUNKS + 4, k],
            device_id=(lax.rem(dp + k, parts), me), device_id_type=MESH)

    barrier = pltpu.get_barrier_semaphore()

    def greet(near, order):
        pl.semaphore_signal(barrier, inc=1, device_id=(dp, partner(near, order)), device_id_type=MESH)

    each(greet)
    for k in range(1, parts):
        pl.semaphore_signal(barrier, inc=1, device_id=(lax.rem(dp + k, parts), me), device_id_type=MESH)

    topk, tb_local = dev_ref.shape
    lane = lax.broadcasted_iota(jnp.int32, (1, LANES), 1)
    slot_owner = jnp.zeros((1, LANES), jnp.int32)
    for owner in range(1, owners + 1):
        slot_owner = slot_owner + jnp.where(lane >= owner * most, 1, 0)
    slot_place = lane - slot_owner * most

    def route(b, carry):
        count, edge_of, codes = carry
        for k in range(topk):
            hit = slot_owner == dev_ref[k, b]
            here = jnp.logical_and(hit, count == slot_place)
            edge_of = jnp.where(here, b * topk + k, edge_of)
            codes = jnp.where(here, slot_ref[k, b], codes)
            count = count + jnp.where(hit, 1, 0)
        return count, edge_of, codes

    none = jnp.zeros((1, LANES), jnp.int32)
    _, edge_of, codes = lax.fori_loop(0, tb_local, route, (none, none, none - 1))
    edges[...] = edge_of
    own_codes[...] = codes
    fetches = [pltpu.make_async_copy(edges, edges_smem, local.at[2]),
               pltpu.make_async_copy(own_codes, own_codes_smem, local.at[3])]
    for fetch in fetches:
        fetch.start()

    row = lax.broadcasted_iota(jnp.int32, (2 * LANES, LANES), 0)
    side = lax.broadcasted_iota(jnp.int32, (2 * LANES, LANES), 1) >= BLK
    for parity in range(2):
        low_part = jnp.logical_and(row >= parity * BLK, row < (parity + 1) * BLK)
        high_part = jnp.logical_and(row >= LANES + parity * BLK, row < LANES + (parity + 1) * BLK)
        kept = jnp.where(side, jnp.where(high_part, 1.0, 0.0), jnp.where(low_part, 1.0, 0.0))
        masks[parity] = kept.astype(jnp.bfloat16)

    pairs = mentor_ref.shape[1] // LANES
    high = mentor_ref[:, :LANES]
    for pair in range(1, pairs):
        high = jnp.maximum(high, mentor_ref[:, pair * LANES:(pair + 1) * LANES])
    teacher_high = jnp.max(high.astype(jnp.float32), axis=1, keepdims=True) / float(SMOOTHING_HEAT)

    def exp_pair(j, total):
        x = mentor_ref[:, pl.ds(pl.multiple_of(j * LANES, LANES), LANES)].astype(jnp.float32)
        e = jnp.exp(x / float(SMOOTHING_HEAT) - teacher_high)
        rounded = e.astype(jnp.bfloat16)
        exps[j] = jnp.concatenate([rounded[:half], rounded[half:]], axis=1)
        return total + e

    teacher_sum = lax.fori_loop(0, pairs, exp_pair, jnp.zeros((row_count, LANES), jnp.float32))
    mass[...] = jnp.zeros((half, LANES), jnp.float32)
    for fetch in fetches:
        fetch.wait()

    def fill_slots(near, order):
        peer = partner(near, order)
        for at in range(most):
            edge = edges_smem[0, peer * most + at]
            weight = weight_ref[edge]
            rhs = jnp.concatenate([weight] * 4, axis=0) * masks[lax.rem(edge // topk, 2)]
            term = jnp.dot(exps[edge // (2 * topk)], rhs, preferred_element_type=jnp.float32).astype(jnp.bfloat16)
            for chunk in range(CHUNKS):
                out[chunk, near * OUTER + order, at] = term[chunk * rows:(chunk + 1) * rows]
            used = jnp.where(own_codes_smem[0, peer * most + at] >= 0, 1.0, 0.0)
            mass[...] = mass[...] + term.astype(jnp.float32) * used

    pl.semaphore_wait(barrier, owners + parts - 2)

    def send_first(near, order):
        fill_slots(near, order)
        blocks(0, near, order).start()

    for order in range(1, OUTER):
        send_first(0, order)
    each(lambda near, order: slot_codes(near, order).start())
    rest(send_first)
    fill_slots(0, 0)
    filled = mass[...]
    target_mass = jnp.concatenate([
        jnp.sum(jnp.where(low, filled, 0.0), axis=1, keepdims=True),
        jnp.sum(jnp.where(low, 0.0, filled), axis=1, keepdims=True),
    ], axis=0)
    columns_to_row([teacher_high, jnp.sum(teacher_sum, axis=1, keepdims=True), target_mass], stats)
    each(lambda near, order: teacher_stats(near, order).start())

    teacher_table[0] = stats[...]
    code_table[0] = own_codes[...]

    def tile_of(j):
        return learner_ref[:, pl.ds(pl.multiple_of(j * LANES, LANES), LANES)]

    high = lax.fori_loop(1, tiles, lambda j, h: jnp.maximum(h, tile_of(j)), learner_ref[:, :LANES])
    high = jnp.max(high.astype(jnp.float32), axis=1, keepdims=True) / float(SMOOTHING_HEAT)

    def add_exp(j, total):
        return total + jnp.exp(tile_of(j).astype(jnp.float32) / float(SMOOTHING_HEAT) - high)

    total = lax.fori_loop(0, tiles, add_exp, jnp.zeros((row_count, LANES), jnp.float32))
    total = jnp.sum(total, axis=1, keepdims=True)
    columns_to_row([high, total], message)
    student_table[0] = message[...]
    each(lambda near, order: student_stats(near, order).start())
    for chunk in range(1, CHUNKS):
        each(lambda near, order: blocks(chunk, near, order).start())

    each(lambda near, order: slot_codes(near, order).wait())
    fetch = pltpu.make_async_copy(code_table, code_smem, local.at[0])
    fetch.start()
    fetch.wait()

    def note(q, last):
        history[pl.ds(q, 1), :] = last
        code = code_smem[q // most, 0, me * most + lax.rem(q, most)]
        return jnp.where(lane == code, q, last)

    last = lax.fori_loop(0, slots, note, jnp.full((1, LANES), slots, jnp.int32))
    history[pl.ds(slots, 1), :] = last
    fetch = pltpu.make_async_copy(history, history_smem, local.at[1])
    fetch.start()
    for chunk in range(CHUNKS):
        sums[chunk, slots] = jnp.zeros((rows, LANES), jnp.float32)

    each(lambda near, order: teacher_stats(near, order).wait())
    teacher_high, teacher_sum, teacher_mass = (
        teacher_table[:, 0, at * row_count:(at + 1) * row_count] for at in range(TEACHER_STATS))
    teacher_scale = jnp.exp(teacher_high - jnp.max(teacher_high, axis=0, keepdims=True))
    weight = teacher_scale / jnp.sum(teacher_sum * teacher_scale, axis=0, keepdims=True)
    target_total = jnp.sum(teacher_mass * weight, axis=0, keepdims=True)
    fill = jnp.zeros((LANES - owners - 1, row_count), jnp.float32)
    columns = jnp.transpose(jnp.concatenate([weight, target_total, fill], axis=0))
    for source in range(owners):
        column = columns[:, source:source + 1]
        scale[source] = jnp.where(low, column[:half], column[half:])
    target_total = columns[:, owners:owners + 1] * vocab_width
    fetch.wait()

    def add_blocks(chunk, slot, source_ref, index):
        at_rows = pl.ds(chunk * rows, rows)
        for at in range(most):
            q = slot * most + at
            code = code_smem[slot, 0, me * most + at]
            earlier = sums[chunk, history_smem[q, jnp.maximum(code, 0)]]
            sums[chunk, q] = earlier + source_ref[chunk, index, at].astype(jnp.float32) * scale[slot, at_rows, :]

    def gather(chunk):
        add_blocks(chunk, 0, out, 0)

        def take(near, order):
            blocks(chunk, near, order).wait()
            slot = near * OUTER + order
            add_blocks(chunk, slot, received, slot)

        each(take)

    def chunk_rows(chunk, column):
        top = chunk * rows
        return jnp.concatenate([column[top:top + rows], column[half + top:half + top + rows]], axis=0)

    def tile(chunk, j):
        first = sums[chunk, history_smem[slots, 2 * j]]
        second = sums[chunk, history_smem[slots, 2 * j + 1]]
        target = jnp.concatenate([
            jnp.where(low_rows, first, pltpu.roll(second, BLK, 1)),
            jnp.where(low_rows, pltpu.roll(first, BLK, 1), second),
        ], axis=0)
        at = pl.ds(pl.multiple_of(j * LANES, LANES), LANES)
        top = pl.ds(chunk * rows, rows)
        bottom = pl.ds(half + chunk * rows, rows)
        logits = jnp.concatenate([learner_ref[top, at], learner_ref[bottom, at]], axis=0).astype(jnp.float32)
        return target, logits / float(SMOOTHING_HEAT), at, top, bottom

    def add_loss(chunk, loss):
        lse_rows = chunk_rows(chunk, lse)

        def body(j, loss):
            target, logits, _, _, _ = tile(chunk, j)
            return loss + jnp.where(target > 0.0, target * (jnp.log(target) - (logits - lse_rows)), 0.0)

        return lax.fori_loop(0, tiles, body, loss)

    def write_gradient(chunk, first, end):
        lse_rows, total_rows = chunk_rows(chunk, lse), chunk_rows(chunk, target_total)

        def body(j, carry):
            target, logits, at, top, bottom = tile(chunk, j)
            grad = (total_rows * jnp.exp(logits - lse_rows) - vocab_width * target).astype(jnp.bfloat16)
            grad_ref[top, at] = grad[:rows]
            grad_ref[bottom, at] = grad[rows:]
            return carry

        lax.fori_loop(first, end, body, 0)

    gather(0)
    each(lambda near, order: student_stats(near, order).wait())
    student_high, student_sum = (
        student_table[:, 0, at * row_count:(at + 1) * row_count] for at in range(STUDENT_STATS))
    top = jnp.max(student_high, axis=0, keepdims=True)
    lse = top + jnp.log(jnp.sum(student_sum * jnp.exp(student_high - top), axis=0, keepdims=True))
    lse = jnp.transpose(jnp.concatenate([lse, jnp.zeros((LANES - 1, row_count), jnp.float32)], axis=0))[:, :1]

    loss = jnp.zeros((2 * rows, LANES), jnp.float32)
    for chunk in range(CHUNKS):
        if chunk:
            gather(chunk)
        loss = add_loss(chunk, loss)
        if chunk < CHUNKS - 1:
            write_gradient(chunk, 0, tiles)

    loss = jnp.sum(loss.reshape(2 * rows // 8, 8, LANES), axis=0)
    part_loss[...] = loss
    for k in range(1, parts):
        part_copy(k).start()
    part_table[dp] = loss
    write_gradient(CHUNKS - 1, 0, tiles // 2)
    for k in range(1, parts):
        part_copy(k).wait()
    loss = jnp.sum(part_table[...], axis=0)
    loss_message[...] = loss
    each(lambda near, order: losses(near, order).start())
    loss_table[0] = loss
    write_gradient(CHUNKS - 1, tiles // 2, tiles)
    each(lambda near, order: losses(near, order).wait())
    totals = jnp.sum(jnp.sum(loss_table[...], axis=1), axis=1, keepdims=True)
    loss_ref[...] = jnp.sum(totals, axis=0, keepdims=True) * loss_scale


def per_device(mentor_score_matrix, learner_score_matrix, align_dev, align_slot, align_weight):
    parts, owners = lax.axis_size("dp"), lax.axis_size("vocab")
    row_count, _ = mentor_score_matrix.shape
    rows = row_count // (2 * CHUNKS)
    tb_local, topk = align_dev.shape
    most = max(2, 3 * tb_local * topk // (2 * owners))
    width = learner_score_matrix.shape[1]
    vmem = pl.BlockSpec(memory_space=pltpu.VMEM)
    smem = pl.BlockSpec(memory_space=pltpu.SMEM)

    weight = align_weight.reshape(tb_local * topk, BLK, BLK)
    weight = jnp.concatenate([weight, weight], axis=2)

    loss_scale = float(SMOOTHING_HEAT) * float(SMOOTHING_HEAT) / float(row_count * parts)
    slots = owners * most
    history_rows = (slots // 8 + 1) * 8
    small = pltpu.VMEM((8, LANES), jnp.float32)
    scaled_grad, loss = pl.pallas_call(
        functools.partial(student_kernel, parts, owners, most, loss_scale),
        out_shape=(
            jax.ShapeDtypeStruct((row_count, width), jnp.bfloat16),
            jax.ShapeDtypeStruct((1, 1), jnp.float32),
        ),
        in_specs=[smem, smem, vmem, vmem, vmem],
        out_specs=(vmem, vmem),
        scratch_shapes=[
            pltpu.VMEM((mentor_score_matrix.shape[1] // LANES, CHUNKS * rows, 2 * LANES), jnp.bfloat16),
            pltpu.VMEM((2, 2 * LANES, LANES), jnp.bfloat16),
            pltpu.VMEM((CHUNKS * rows, LANES), jnp.float32),
            pltpu.VMEM((1, LANES), jnp.int32),
            pltpu.SMEM((1, LANES), jnp.int32),
            pltpu.VMEM((1, LANES), jnp.int32),
            pltpu.SMEM((1, LANES), jnp.int32),
            pltpu.VMEM((CHUNKS, owners, most, rows, LANES), jnp.bfloat16),
            pltpu.VMEM((1, TEACHER_STATS * row_count), jnp.float32),
            pltpu.VMEM((CHUNKS, owners, most, rows, LANES), jnp.bfloat16),
            pltpu.VMEM((CHUNKS, slots + 1, rows, LANES), jnp.float32),
            pltpu.VMEM((owners, CHUNKS * rows, LANES), jnp.float32),
            pltpu.VMEM((1, STUDENT_STATS * row_count), jnp.float32),
            pltpu.VMEM((owners, 1, TEACHER_STATS * row_count), jnp.float32),
            pltpu.VMEM((owners, 1, STUDENT_STATS * row_count), jnp.float32),
            pltpu.VMEM((owners, 1, LANES), jnp.int32),
            pltpu.SMEM((owners, 1, LANES), jnp.int32),
            pltpu.VMEM((history_rows, LANES), jnp.int32),
            pltpu.SMEM((history_rows, LANES), jnp.int32),
            small,
            pltpu.VMEM((parts, 8, LANES), jnp.float32),
            small,
            pltpu.VMEM((owners, 8, LANES), jnp.float32),
            pltpu.SemaphoreType.DMA((CHUNKS + 5, owners)),
            pltpu.SemaphoreType.DMA((CHUNKS + 5, owners)),
            pltpu.SemaphoreType.DMA((4,)),
        ],
        compiler_params=pltpu.CompilerParams(
            collective_id=0, has_side_effects=True, vmem_limit_bytes=VMEM_BYTES),
        name="distillation",
    )(align_dev.T, align_slot.T, mentor_score_matrix, weight, learner_score_matrix)
    return scaled_grad, loss[0, 0]


def solution(mesh):
    in_specs = (
        P("dp", "vocab"),
        P("dp", "vocab"),
        P("vocab", None),
        P("vocab", None),
        P("vocab", None, None),
    )
    out_specs = (P("dp", "vocab"), P())
    return jax.shard_map(
        per_device, mesh=mesh, in_specs=in_specs, out_specs=out_specs, check_vma=False
    )
```

```python
import functools

import jax
import jax.numpy as jnp
from jax import lax
from jax.experimental import pallas as pl
from jax.experimental.pallas import tpu as pltpu
from jax.sharding import PartitionSpec as P

BLK = 64
SMOOTHING_HEAT = 2
LANES = 128
CHUNKS = 2
TEACHER_STATS = 3
STUDENT_STATS = 2
OUTER = 4
FAR = (0, 2, 1, 3)
VMEM_BYTES = 24 * 1024 * 1024
MESH = pl.DeviceIdType.MESH


def low_lanes(shape):
    return lax.broadcasted_iota(jnp.int32, shape, len(shape) - 1) < BLK


def columns_to_row(columns, row_ref):
    rows = columns[0].shape[0]
    lane = lax.broadcasted_iota(jnp.int32, (rows, LANES), 1)
    table = jnp.zeros((rows, LANES), jnp.float32)
    for at, column in enumerate(columns):
        table = jnp.where(lane == at, column, table)
    table = jnp.transpose(table)
    for at in range(len(columns)):
        row_ref[:, at * rows:(at + 1) * rows] = table[at:at + 1]


def outer_partner(outer, far):
    return (outer, outer + 1 - 2 * lax.rem(outer, 2), lax.rem(outer + 2, OUTER), OUTER - 1 - outer)[far]


def student_kernel(parts, owners, most, loss_scale,
                   dev_ref, slot_ref, mentor_ref, weight_ref, learner_ref, grad_ref, loss_ref,
                   exps, masks, mass, edges, edges_smem, own_codes, own_codes_smem, out, stats,
                   received, sums, scale, message, teacher_table, student_table, code_table, code_smem,
                   history, history_smem, part_loss, part_table, loss_message, loss_table,
                   send, recv, local):
    dp, me = lax.axis_index("dp"), lax.axis_index("vocab")
    row_count, width = learner_ref.shape
    half = row_count // 2
    rows = half // CHUNKS
    tiles = width // LANES
    slots = owners * most
    inner = owners // OUTER
    vocab_width = float(width * owners)
    low = low_lanes((half, LANES))
    low_rows = low_lanes((rows, LANES))

    def partner(near, order):
        return outer_partner(me // inner, FAR[order]) * inner + lax.rem(lax.rem(me, inner) + near, inner)

    def copy_to(kind, near, order, src, dst):
        slot = near * OUTER + order
        return pltpu.make_async_remote_copy(
            src_ref=src, dst_ref=dst.at[slot], send_sem=send.at[kind, slot], recv_sem=recv.at[kind, slot],
            device_id=(dp, partner(near, order)), device_id_type=MESH)

    def blocks(chunk, near, order):
        return copy_to(chunk, near, order, out.at[chunk, near * OUTER + order], received.at[chunk])

    def teacher_stats(near, order):
        return copy_to(CHUNKS, near, order, stats, teacher_table)

    def slot_codes(near, order):
        return copy_to(CHUNKS + 1, near, order, own_codes, code_table)

    def student_stats(near, order):
        return copy_to(CHUNKS + 2, near, order, message, student_table)

    def losses(near, order):
        return copy_to(CHUNKS + 3, near, order, loss_message, loss_table)

    def each(action):
        for order in range(1, OUTER):
            action(0, order)
        rest(action)

    def rest(action):
        def body(near, carry):
            for order in range(OUTER):
                action(near, order)
            return carry

        lax.fori_loop(1, inner, body, 0)

    def part_copy(k):
        return pltpu.make_async_remote_copy(
            src_ref=part_loss, dst_ref=part_table.at[dp], send_sem=send.at[CHUNKS + 4, k], recv_sem=recv.at[CHUNKS + 4, k],
            device_id=(lax.rem(dp + k, parts), me), device_id_type=MESH)

    barrier = pltpu.get_barrier_semaphore()

    def greet(near, order):
        pl.semaphore_signal(barrier, inc=1, device_id=(dp, partner(near, order)), device_id_type=MESH)

    each(greet)
    for k in range(1, parts):
        pl.semaphore_signal(barrier, inc=1, device_id=(lax.rem(dp + k, parts), me), device_id_type=MESH)

    topk, tb_local = dev_ref.shape
    lane = lax.broadcasted_iota(jnp.int32, (1, LANES), 1)
    slot_owner = jnp.zeros((1, LANES), jnp.int32)
    for owner in range(1, owners + 1):
        slot_owner = slot_owner + jnp.where(lane >= owner * most, 1, 0)
    slot_place = lane - slot_owner * most

    def route(b, carry):
        count, edge_of, codes = carry
        for k in range(topk):
            hit = slot_owner == dev_ref[k, b]
            here = jnp.logical_and(hit, count == slot_place)
            edge_of = jnp.where(here, b * topk + k, edge_of)
            codes = jnp.where(here, slot_ref[k, b], codes)
            count = count + jnp.where(hit, 1, 0)
        return count, edge_of, codes

    none = jnp.zeros((1, LANES), jnp.int32)
    _, edge_of, codes = lax.fori_loop(0, tb_local, route, (none, none, none - 1))
    edges[...] = edge_of
    own_codes[...] = codes
    fetches = [pltpu.make_async_copy(edges, edges_smem, local.at[2]),
               pltpu.make_async_copy(own_codes, own_codes_smem, local.at[3])]
    for fetch in fetches:
        fetch.start()

    row = lax.broadcasted_iota(jnp.int32, (2 * LANES, LANES), 0)
    side = lax.broadcasted_iota(jnp.int32, (2 * LANES, LANES), 1) >= BLK
    for parity in range(2):
        low_part = jnp.logical_and(row >= parity * BLK, row < (parity + 1) * BLK)
        high_part = jnp.logical_and(row >= LANES + parity * BLK, row < LANES + (parity + 1) * BLK)
        kept = jnp.where(side, jnp.where(high_part, 1.0, 0.0), jnp.where(low_part, 1.0, 0.0))
        masks[parity] = kept.astype(jnp.bfloat16)

    pairs = mentor_ref.shape[1] // LANES
    high = mentor_ref[:, :LANES]
    for pair in range(1, pairs):
        high = jnp.maximum(high, mentor_ref[:, pair * LANES:(pair + 1) * LANES])
    teacher_high = jnp.max(high.astype(jnp.float32), axis=1, keepdims=True) / float(SMOOTHING_HEAT)

    def exp_pair(j, total):
        x = mentor_ref[:, pl.ds(pl.multiple_of(j * LANES, LANES), LANES)].astype(jnp.float32)
        e = jnp.exp(x / float(SMOOTHING_HEAT) - teacher_high)
        rounded = e.astype(jnp.bfloat16)
        exps[j] = jnp.concatenate([rounded[:half], rounded[half:]], axis=1)
        return total + e

    teacher_sum = lax.fori_loop(0, pairs, exp_pair, jnp.zeros((row_count, LANES), jnp.float32))
    mass[...] = jnp.zeros((half, LANES), jnp.float32)
    for fetch in fetches:
        fetch.wait()

    def fill_slots(near, order):
        peer = partner(near, order)
        for at in range(most):
            edge = edges_smem[0, peer * most + at]
            weight = jnp.concatenate([weight_ref[edge]] * 2, axis=1)
            rhs = jnp.concatenate([weight] * 4, axis=0) * masks[lax.rem(edge // topk, 2)]
            term = jnp.dot(exps[edge // (2 * topk)], rhs, preferred_element_type=jnp.float32).astype(jnp.bfloat16)
            for chunk in range(CHUNKS):
                out[chunk, near * OUTER + order, at] = term[chunk * rows:(chunk + 1) * rows]
            used = jnp.where(own_codes_smem[0, peer * most + at] >= 0, 1.0, 0.0)
            mass[...] = mass[...] + term.astype(jnp.float32) * used

    pl.semaphore_wait(barrier, owners + parts - 2)

    def send_first(near, order):
        fill_slots(near, order)
        blocks(0, near, order).start()

    for order in range(1, OUTER):
        send_first(0, order)
    each(lambda near, order: slot_codes(near, order).start())
    rest(send_first)
    fill_slots(0, 0)
    filled = mass[...]
    target_mass = jnp.concatenate([
        jnp.sum(jnp.where(low, filled, 0.0), axis=1, keepdims=True),
        jnp.sum(jnp.where(low, 0.0, filled), axis=1, keepdims=True),
    ], axis=0)
    columns_to_row([teacher_high, jnp.sum(teacher_sum, axis=1, keepdims=True), target_mass], stats)
    each(lambda near, order: teacher_stats(near, order).start())

    teacher_table[0] = stats[...]
    code_table[0] = own_codes[...]

    def tile_of(j):
        return learner_ref[:, pl.ds(pl.multiple_of(j * LANES, LANES), LANES)]

    high = lax.fori_loop(1, tiles, lambda j, h: jnp.maximum(h, tile_of(j)), learner_ref[:, :LANES])
    high = jnp.max(high.astype(jnp.float32), axis=1, keepdims=True) / float(SMOOTHING_HEAT)

    def add_exp(j, total):
        return total + jnp.exp(tile_of(j).astype(jnp.float32) / float(SMOOTHING_HEAT) - high)

    total = lax.fori_loop(0, tiles, add_exp, jnp.zeros((row_count, LANES), jnp.float32))
    total = jnp.sum(total, axis=1, keepdims=True)
    columns_to_row([high, total], message)
    student_table[0] = message[...]
    each(lambda near, order: student_stats(near, order).start())
    for chunk in range(1, CHUNKS):
        each(lambda near, order: blocks(chunk, near, order).start())

    each(lambda near, order: slot_codes(near, order).wait())
    fetch = pltpu.make_async_copy(code_table, code_smem, local.at[0])
    fetch.start()
    fetch.wait()

    def note(q, last):
        history[pl.ds(q, 1), :] = last
        code = code_smem[q // most, 0, me * most + lax.rem(q, most)]
        return jnp.where(lane == code, q, last)

    last = lax.fori_loop(0, slots, note, jnp.full((1, LANES), slots, jnp.int32))
    history[pl.ds(slots, 1), :] = last
    fetch = pltpu.make_async_copy(history, history_smem, local.at[1])
    fetch.start()
    for chunk in range(CHUNKS):
        sums[chunk, slots] = jnp.zeros((rows, LANES), jnp.float32)

    each(lambda near, order: teacher_stats(near, order).wait())
    teacher_high, teacher_sum, teacher_mass = (
        teacher_table[:, 0, at * row_count:(at + 1) * row_count] for at in range(TEACHER_STATS))
    teacher_scale = jnp.exp(teacher_high - jnp.max(teacher_high, axis=0, keepdims=True))
    weight = teacher_scale / jnp.sum(teacher_sum * teacher_scale, axis=0, keepdims=True)
    target_total = jnp.sum(teacher_mass * weight, axis=0, keepdims=True)
    fill = jnp.zeros((LANES - owners - 1, row_count), jnp.float32)
    columns = jnp.transpose(jnp.concatenate([weight, target_total, fill], axis=0))
    for source in range(owners):
        column = columns[:, source:source + 1]
        scale[source] = jnp.where(low, column[:half], column[half:])
    target_total = columns[:, owners:owners + 1] * vocab_width
    fetch.wait()

    def add_blocks(chunk, slot, source_ref, index):
        at_rows = pl.ds(chunk * rows, rows)
        for at in range(most):
            q = slot * most + at
            code = code_smem[slot, 0, me * most + at]
            earlier = sums[chunk, history_smem[q, jnp.maximum(code, 0)]]
            sums[chunk, q] = earlier + source_ref[chunk, index, at].astype(jnp.float32) * scale[slot, at_rows, :]

    def gather(chunk):
        add_blocks(chunk, 0, out, 0)

        def take(near, order):
            blocks(chunk, near, order).wait()
            slot = near * OUTER + order
            add_blocks(chunk, slot, received, slot)

        each(take)

    def chunk_rows(chunk, column):
        top = chunk * rows
        return jnp.concatenate([column[top:top + rows], column[half + top:half + top + rows]], axis=0)

    def tile(chunk, j):
        first = sums[chunk, history_smem[slots, 2 * j]]
        second = sums[chunk, history_smem[slots, 2 * j + 1]]
        target = jnp.concatenate([
            jnp.where(low_rows, first, pltpu.roll(second, BLK, 1)),
            jnp.where(low_rows, pltpu.roll(first, BLK, 1), second),
        ], axis=0)
        at = pl.ds(pl.multiple_of(j * LANES, LANES), LANES)
        top = pl.ds(chunk * rows, rows)
        bottom = pl.ds(half + chunk * rows, rows)
        logits = jnp.concatenate([learner_ref[top, at], learner_ref[bottom, at]], axis=0).astype(jnp.float32)
        return target, logits / float(SMOOTHING_HEAT), at, top, bottom

    def add_loss(chunk, loss):
        lse_rows = chunk_rows(chunk, lse)

        def body(j, loss):
            target, logits, _, _, _ = tile(chunk, j)
            return loss + jnp.where(target > 0.0, target * (jnp.log(target) - (logits - lse_rows)), 0.0)

        return lax.fori_loop(0, tiles, body, loss)

    def write_gradient(chunk, first, end):
        lse_rows, total_rows = chunk_rows(chunk, lse), chunk_rows(chunk, target_total)

        def body(j, carry):
            target, logits, at, top, bottom = tile(chunk, j)
            grad = (total_rows * jnp.exp(logits - lse_rows) - vocab_width * target).astype(jnp.bfloat16)
            grad_ref[top, at] = grad[:rows]
            grad_ref[bottom, at] = grad[rows:]
            return carry

        lax.fori_loop(first, end, body, 0)

    gather(0)
    each(lambda near, order: student_stats(near, order).wait())
    student_high, student_sum = (
        student_table[:, 0, at * row_count:(at + 1) * row_count] for at in range(STUDENT_STATS))
    top = jnp.max(student_high, axis=0, keepdims=True)
    lse = top + jnp.log(jnp.sum(student_sum * jnp.exp(student_high - top), axis=0, keepdims=True))
    lse = jnp.transpose(jnp.concatenate([lse, jnp.zeros((LANES - 1, row_count), jnp.float32)], axis=0))[:, :1]

    loss = jnp.zeros((2 * rows, LANES), jnp.float32)
    for chunk in range(CHUNKS):
        if chunk:
            gather(chunk)
        loss = add_loss(chunk, loss)
        if chunk < CHUNKS - 1:
            write_gradient(chunk, 0, tiles)

    loss = jnp.sum(loss.reshape(2 * rows // 8, 8, LANES), axis=0)
    part_loss[...] = loss
    for k in range(1, parts):
        part_copy(k).start()
    part_table[dp] = loss
    write_gradient(CHUNKS - 1, 0, tiles // 2)
    for k in range(1, parts):
        part_copy(k).wait()
    loss = jnp.sum(part_table[...], axis=0)
    loss_message[...] = loss
    each(lambda near, order: losses(near, order).start())
    loss_table[0] = loss
    write_gradient(CHUNKS - 1, tiles // 2, tiles)
    each(lambda near, order: losses(near, order).wait())
    totals = jnp.sum(jnp.sum(loss_table[...], axis=1), axis=1, keepdims=True)
    loss_ref[...] = jnp.sum(totals, axis=0, keepdims=True) * loss_scale


def per_device(mentor_score_matrix, learner_score_matrix, align_dev, align_slot, align_weight):
    parts, owners = lax.axis_size("dp"), lax.axis_size("vocab")
    row_count, _ = mentor_score_matrix.shape
    rows = row_count // (2 * CHUNKS)
    tb_local, topk = align_dev.shape
    most = max(2, 3 * tb_local * topk // (2 * owners))
    width = learner_score_matrix.shape[1]
    vmem = pl.BlockSpec(memory_space=pltpu.VMEM)
    smem = pl.BlockSpec(memory_space=pltpu.SMEM)

    weight = align_weight.reshape(tb_local * topk, BLK, BLK)

    loss_scale = float(SMOOTHING_HEAT) * float(SMOOTHING_HEAT) / float(row_count * parts)
    slots = owners * most
    history_rows = (slots // 8 + 1) * 8
    small = pltpu.VMEM((8, LANES), jnp.float32)
    scaled_grad, loss = pl.pallas_call(
        functools.partial(student_kernel, parts, owners, most, loss_scale),
        out_shape=(
            jax.ShapeDtypeStruct((row_count, width), jnp.bfloat16),
            jax.ShapeDtypeStruct((1, 1), jnp.float32),
        ),
        in_specs=[smem, smem, vmem, vmem, vmem],
        out_specs=(vmem, vmem),
        scratch_shapes=[
            pltpu.VMEM((mentor_score_matrix.shape[1] // LANES, CHUNKS * rows, 2 * LANES), jnp.bfloat16),
            pltpu.VMEM((2, 2 * LANES, LANES), jnp.bfloat16),
            pltpu.VMEM((CHUNKS * rows, LANES), jnp.float32),
            pltpu.VMEM((1, LANES), jnp.int32),
            pltpu.SMEM((1, LANES), jnp.int32),
            pltpu.VMEM((1, LANES), jnp.int32),
            pltpu.SMEM((1, LANES), jnp.int32),
            pltpu.VMEM((CHUNKS, owners, most, rows, LANES), jnp.bfloat16),
            pltpu.VMEM((1, TEACHER_STATS * row_count), jnp.float32),
            pltpu.VMEM((CHUNKS, owners, most, rows, LANES), jnp.bfloat16),
            pltpu.VMEM((CHUNKS, slots + 1, rows, LANES), jnp.float32),
            pltpu.VMEM((owners, CHUNKS * rows, LANES), jnp.float32),
            pltpu.VMEM((1, STUDENT_STATS * row_count), jnp.float32),
            pltpu.VMEM((owners, 1, TEACHER_STATS * row_count), jnp.float32),
            pltpu.VMEM((owners, 1, STUDENT_STATS * row_count), jnp.float32),
            pltpu.VMEM((owners, 1, LANES), jnp.int32),
            pltpu.SMEM((owners, 1, LANES), jnp.int32),
            pltpu.VMEM((history_rows, LANES), jnp.int32),
            pltpu.SMEM((history_rows, LANES), jnp.int32),
            small,
            pltpu.VMEM((parts, 8, LANES), jnp.float32),
            small,
            pltpu.VMEM((owners, 8, LANES), jnp.float32),
            pltpu.SemaphoreType.DMA((CHUNKS + 5, owners)),
            pltpu.SemaphoreType.DMA((CHUNKS + 5, owners)),
            pltpu.SemaphoreType.DMA((4,)),
        ],
        compiler_params=pltpu.CompilerParams(
            collective_id=0, has_side_effects=True, vmem_limit_bytes=VMEM_BYTES),
        name="distillation",
    )(align_dev.T, align_slot.T, mentor_score_matrix, weight, learner_score_matrix)
    return scaled_grad, loss[0, 0]


def solution(mesh):
    in_specs = (
        P("dp", "vocab"),
        P("dp", "vocab"),
        P("vocab", None),
        P("vocab", None),
        P("vocab", None, None),
    )
    out_specs = (P("dp", "vocab"), P())
    return jax.shard_map(
        per_device, mesh=mesh, in_specs=in_specs, out_specs=out_specs, check_vma=False
    )
```
